256 devices in a mesh: seq: 16 (over z, core), fsdp: 16 (over y, x).
Axes of the slice: x: 4, y: 4, z: 8, core: 2. Of those that a mesh axis runs over, the one named last changes fastest.
Arguments:
- qkv_raw: bfloat16 [16, 2048, 4096], P('fsdp', 'seq'), may hold values from -6 to 6
- output_gate: bfloat16 [16, 2048, 2048], P('fsdp', 'seq'), may hold values from -6 to 6
- decay_codes: int32 [16, 16, 2048], P('fsdp', None, 'seq'), may hold values from 0 to 559
- beta_codes: int32 [16, 16, 2048], P('fsdp', None, 'seq'), may hold values from 32 to 319
- conv_weight: float32 [4, 4096], replicated, may hold values from -3 to 3
- decay_scale_log: float32 [16], replicated
- decay_bias: float32 [16], replicated, may hold values from -0.5 to 0.5
- norm_gain: float32 [128], replicated, may hold values from 0.5 to 1.5
- out_weight: bfloat16 [2048, 2048], P('fsdp'), may hold values from -0.125 to 0.125
Outputs:
- layer_out: bfloat16 [16, 2048, 2048], P('fsdp', 'seq')
The draws below stay inside these ranges and needn't reach their ends.
All inputs are finite; a program needn't handle non-finite values.
Results may differ from the reference program's by a relative error of at most 0.0049.
Values may be sent and summed in bfloat16 or wider, within the bound.
No kernel may reach another device: no remote copies, remote signals or barrier semaphores. Data moves between devices by JAX's collectives and lax.ppermute only.
A program may use at most 128 MiB of HBM per device.

```python
import math
import jax
import jax.numpy as jnp
from jax import lax

D = 2048
KH = 8
VH = 16
DK = 128
DV = 128
KERNEL = 4
BLOCK = 64
SEQUENCE_LENGTH = 2048
SEQS = 16
QKV = 4096
VDIM = 2048


def draw_decay_codes(key, part):
    base_floor = int(32.0 * (16.0 - math.log(SEQUENCE_LENGTH))) - 32
    first_key, second_key_rows, third_key_rows, fourth_key_rows = jax.random.split(jax.random.fold_in(key, 11), 4)
    draw_shape = (SEQS, VH, SEQUENCE_LENGTH)
    baseline_codes = jax.random.randint(first_key, draw_shape, base_floor, base_floor + 64)
    lowered_seqs = jax.random.permutation(fourth_key_rows, SEQS) < (SEQS + 1) // 2
    baseline_codes = baseline_codes - jnp.where(lowered_seqs, 96, 0).astype(jnp.int32)[:, None, None]
    baseline_codes = jnp.maximum(baseline_codes, 0)
    spike_codes = jax.random.randint(second_key_rows, draw_shape, 528, 560)
    spike_mask = jax.random.randint(third_key_rows, draw_shape, 0, SEQUENCE_LENGTH) < 2
    draw_codes = jnp.where(spike_mask, spike_codes, baseline_codes)
    position = jax.lax.broadcasted_iota(jnp.int32, draw_shape, 2)
    draw_codes = jnp.where(position == 0, 0, draw_codes)
    return draw_codes.astype(jnp.int32)


def draw_beta_codes(key, part):
    first_key, second_key_rows, third_key_rows = jax.random.split(jax.random.fold_in(key, 23), 3)
    draw_shape = (SEQS, VH, SEQUENCE_LENGTH)
    baseline_codes = jax.random.randint(first_key, draw_shape, 32, 128)
    strong = jax.random.randint(second_key_rows, draw_shape, 256, 320)
    strong_mask = jax.random.randint(third_key_rows, draw_shape, 0, 100) < 1
    return jnp.where(strong_mask, strong, baseline_codes).astype(jnp.int32)


def draw_decay_scale_log(key, part):
    first_key, second_key_rows, third_key_rows, fourth_key_rows = jax.random.split(jax.random.fold_in(key, 37), 4)
    slow_share = 0.5
    slow_mask = jax.random.uniform(first_key, (VH,), jnp.float32) < slow_share
    forced_fast = jax.random.randint(fourth_key_rows, (), 0, VH)
    head_ids = jax.lax.broadcasted_iota(jnp.int32, (VH,), 0)
    slow_mask = jnp.logical_and(slow_mask, head_ids != forced_fast)
    slow_value = math.log(0.1) + jax.random.uniform(second_key_rows, (VH,), jnp.float32) * math.log(3.5)
    fast_value = math.log(SEQUENCE_LENGTH / 47.0) + jax.random.uniform(third_key_rows, (VH,), jnp.float32, -0.35, 0.35)
    return jnp.where(slow_mask, slow_value, fast_value).astype(jnp.float32)


def block_scale(key, dims, cuts, least, top_value):
    loudness, own = 1.0, jax.random.fold_in(key, 6)
    for axis_at, parts in cuts:
        draws = jnp.exp(jax.random.uniform(jax.random.fold_in(own, axis_at), (parts,), jnp.float32, least / len(cuts), top_value / len(cuts)))
        loudness = loudness * jnp.repeat(draws, dims[axis_at] // parts).reshape([-1 if axis == axis_at else 1 for axis in range(len(dims))])
    return loudness


def gaussian(key, dims, spread, most, cuts=(), kind=jnp.bfloat16):
    entries = spread * jax.random.normal(key, dims, jnp.float32)
    if cuts:
        entries = entries * block_scale(key, dims, cuts, -0.22, 0.18)
    return jnp.clip(entries, -most, most).astype(kind)


def setup_inputs(seed: int = 0) -> dict:
    key_of = jax.random.split(jax.random.key(seed), 10)
    return {
        "qkv_raw": gaussian(key_of[0], (SEQS, SEQUENCE_LENGTH, QKV), 1.0, 6.0, ((0, 16), (1, 16))),
        "output_gate": gaussian(key_of[1], (SEQS, SEQUENCE_LENGTH, VDIM), 1.0, 6.0, ((0, 16), (1, 16))),
        "decay_codes": draw_decay_codes(jax.random.fold_in(key_of[9], 71), 0),
        "beta_codes": draw_beta_codes(jax.random.fold_in(key_of[9], 71), 0),
        "conv_weight": gaussian(key_of[4], (KERNEL, QKV), 0.5, 3.0, (), jnp.float32),
        "decay_scale_log": draw_decay_scale_log(jax.random.fold_in(key_of[9], 71), 0),
        "decay_bias": jnp.clip(jax.random.uniform(key_of[6], (VH,), jnp.float32, -0.5, 0.5), -0.5, 0.5),
        "norm_gain": jnp.clip(jax.random.uniform(key_of[7], (DV,), jnp.float32, 0.5, 1.5), 0.5, 1.5),
        "out_weight": gaussian(key_of[8], (VDIM, D), VDIM ** -0.5, 0.125, ((0, 16),)),
    }


def product(left, right):
    return jnp.einsum('...ij,...jk->...ik', left, right, precision=lax.Precision.HIGHEST)

def convolve(widened, conv_weight, tok_count):
    total_sum = conv_weight[0][None, :] * widened[0:tok_count]
    for tap_index in range(1, KERNEL):
        total_sum = total_sum + conv_weight[tap_index][None, :] * widened[tap_index:tap_index + tok_count]
    return jax.nn.silu(total_sum)

def prepare(mixed_rows, decay_rows, beta_rows, decay_scale_log, decay_bias):
    tok_count = mixed_rows.shape[0]
    key_width = KH * DK
    queries = mixed_rows[:, :key_width].reshape(tok_count, KH, DK)
    key_vecs = mixed_rows[:, key_width:2 * key_width].reshape(tok_count, KH, DK)
    value_vecs = mixed_rows[:, 2 * key_width:].reshape(tok_count, VH, DV)
    queries = queries / jnp.sqrt(lax.optimization_barrier(jnp.sum(queries * queries, axis=-1, keepdims=True)) + 1e-06) / math.sqrt(DK)
    key_vecs = key_vecs / jnp.sqrt(lax.optimization_barrier(jnp.sum(key_vecs * key_vecs, axis=-1, keepdims=True)) + 1e-06)
    repeat_count = VH // KH
    queries = jnp.repeat(jnp.transpose(queries, (1, 0, 2)), repeat_count, axis=0)
    key_vecs = jnp.repeat(jnp.transpose(key_vecs, (1, 0, 2)), repeat_count, axis=0)
    value_vecs = jnp.transpose(value_vecs, (1, 0, 2))
    blocks = tok_count // BLOCK
    beta_rate = jax.nn.sigmoid(beta_rows.astype(jnp.float32) / 32.0 - 8.0)
    log_decay = -jnp.exp(decay_scale_log)[:, None] * jax.nn.softplus(decay_rows.astype(jnp.float32) / 32.0 - 16.0 + decay_bias[:, None])
    return (queries.reshape(VH, blocks, BLOCK, DK), key_vecs.reshape(VH, blocks, BLOCK, DK), value_vecs.reshape(VH, blocks, BLOCK, DV), beta_rate.reshape(VH, blocks, BLOCK), log_decay.reshape(VH, blocks, BLOCK))

def block_terms(queries, key_vecs, value_vecs, beta_rate, log_decay):
    block_len = key_vecs.shape[-2]
    cumulative = jnp.cumsum(log_decay, axis=-1)
    row_ids = lax.broadcasted_iota(jnp.int32, (block_len, block_len), 0)
    col_ids = lax.broadcasted_iota(jnp.int32, (block_len, block_len), 1)
    inclusive = row_ids >= col_ids
    strict = row_ids > col_ids
    log_gap = cumulative[..., :, None] - cumulative[..., None, :]
    decay_pair = jnp.where(inclusive, jnp.exp(jnp.minimum(log_gap, 0.0)), 0.0)
    key_gram = jnp.einsum('...td,...sd->...ts', key_vecs, key_vecs, precision=lax.Precision.HIGHEST)
    lower_part = jnp.where(strict, beta_rate[..., :, None] * decay_pair * key_gram, 0.0)
    unit_matrix = jnp.eye(block_len, dtype=key_vecs.dtype)
    negated = -lower_part
    inverse = unit_matrix + negated
    power_term = negated
    for counter in range(block_len.bit_length() - 2):
        power_term = product(power_term, power_term)
        inverse = inverse + product(inverse, power_term)
    start_decay = jnp.exp(cumulative)
    right_side = jnp.concatenate([beta_rate[..., None] * value_vecs, (beta_rate * start_decay)[..., None] * key_vecs], axis=-1)
    solved = product(inverse, right_side)
    new_values = solved[..., :DV]
    write_keys = solved[..., DV:]
    query_gram = decay_pair * jnp.einsum('...td,...sd->...ts', queries, key_vecs, precision=lax.Precision.HIGHEST)
    local_out = product(query_gram, new_values)
    state_read = start_decay[..., None] * queries - product(query_gram, write_keys)
    end_decay = jnp.exp(cumulative[..., -1:] - cumulative)
    key_scaled = jnp.swapaxes(end_decay[..., None] * key_vecs, -1, -2)
    unit_keys = jnp.eye(DK, dtype=key_vecs.dtype)
    transit = jnp.exp(cumulative[..., -1])[..., None, None] * unit_keys - product(key_scaled, write_keys)
    state_add = product(key_scaled, new_values)
    return (local_out, state_read, transit, state_add)

def reference(qkv_raw, output_gate, decay_codes, beta_codes, conv_weight, decay_scale_log, decay_bias, norm_gain, out_weight):

    def per_sequence(seq_items):
        raw_rows, gate_rows, decay_rows, beta_rows = seq_items
        length = raw_rows.shape[0]
        widened = jnp.concatenate([jnp.zeros((KERNEL - 1, raw_rows.shape[1]), jnp.float32), raw_rows.astype(jnp.float32)], axis=0)
        mixed_rows = convolve(widened, conv_weight, length)
        queries, key_vecs, value_vecs, beta_rate, log_decay = prepare(mixed_rows, decay_rows, beta_rows, decay_scale_log, decay_bias)
        local_out, state_read, transit, state_add = block_terms(queries, key_vecs, value_vecs, beta_rate, log_decay)

        def advance(state, pieces):
            read_block, transit_block, add_block = pieces
            correction = product(read_block, state)
            state = product(transit_block, state) + add_block
            return (state, correction)
        initial = jnp.zeros((VH, DK, DV), jnp.float32)
        final_state, corrections = lax.scan(advance, initial, (jnp.moveaxis(state_read, 1, 0), jnp.moveaxis(transit, 1, 0), jnp.moveaxis(state_add, 1, 0)))
        heads_out = (local_out + jnp.moveaxis(corrections, 0, 1)).reshape(VH, length, DV)
        square_mean = lax.optimization_barrier(jnp.mean(heads_out * heads_out, axis=-1, keepdims=True))
        gate_heads = jnp.transpose(gate_rows.astype(jnp.float32).reshape(length, VH, DV), (1, 0, 2))
        normed = heads_out / jnp.sqrt(square_mean + 1e-06) * norm_gain * jax.nn.silu(gate_heads)
        normed = jnp.transpose(normed, (1, 0, 2)).reshape(length, VDIM).astype(jnp.bfloat16)
        return jnp.dot(normed, out_weight, preferred_element_type=jnp.float32).astype(jnp.bfloat16)
    return lax.map(per_sequence, (qkv_raw, output_gate, decay_codes, beta_codes))
```

```python
import math

import jax
import jax.numpy as jnp
from jax import lax
from jax.experimental import pallas as pl
from jax.experimental.pallas import tpu as pltpu
from jax.sharding import PartitionSpec as P


CHIPS = 8
SEGMENTS = 16
C = 128
DK = 128
DV = 128
VH = 16
WIDTH = 2048
HALF = 1024
CODES = 4 * C
PIECE = CODES + 16
F32 = jnp.float32
BF16 = jnp.bfloat16


def to_chip(block, distance):
    return lax.ppermute(
        block, "seq", [(i, (i + 2 * distance) % SEGMENTS) for i in range(SEGMENTS)]
    )


def other_core(block):
    return lax.ppermute(block, "seq", [(i, i ^ 1) for i in range(SEGMENTS)])


def dot(left, right):
    return jnp.dot(left, right, preferred_element_type=F32)


def dot_t(left, right):
    return lax.dot_general(
        left, right, (((1,), (1,)), ((), ())), preferred_element_type=F32
    )


def split(value):
    high = value.astype(BF16)
    return high, (value - high.astype(F32)).astype(BF16)


def dot3(left, right):
    lh, ll = left
    rh, rl = right
    return dot(jnp.concatenate([lh, ll], 1), jnp.concatenate([rh, rh], 0)) + dot(lh, rl)


def silu(value):
    return value / (1.0 + jnp.exp(-value))


def pieces_kernel(place, raw, decay, beta, *rest):
    outs, rows = rest[:CHIPS], rest[CHIPS]
    z = place[0]
    rows[...] = jnp.zeros_like(rows)
    for distance in range(CHIPS):
        chip = lax.rem(z + distance, CHIPS)
        out = outs[distance]
        at = pl.multiple_of(chip * DK, DK)
        out[0:C] = raw[:, pl.ds(at, DK)]
        out[C : 2 * C] = raw[:, pl.ds(at + CHIPS * DK, DK)]
        at = pl.multiple_of(chip * 2 * DV, 2 * DV)
        out[2 * C : 3 * C] = raw[:, pl.ds(at + 2 * CHIPS * DK, DV)]
        out[3 * C : 4 * C] = raw[:, pl.ds(at + 2 * CHIPS * DK + DV, DV)]
        for first, codes in ((0, decay), (4, beta)):
            pair = codes[pl.ds(2 * chip, 2), :]
            rows[first : first + 2] = (pair >> 4).astype(F32)
            rows[first + 2 : first + 4] = (pair & 15).astype(F32)
        out[CODES:PIECE] = rows[...].astype(BF16)


def cut_pieces(place, raw, decay, beta):
    vmem = pl.BlockSpec(memory_space=pltpu.VMEM)
    return pl.pallas_call(
        pieces_kernel,
        out_shape=[jax.ShapeDtypeStruct((PIECE, DK), BF16)] * CHIPS,
        in_specs=[pl.BlockSpec(memory_space=pltpu.SMEM), vmem, vmem, vmem],
        out_specs=[vmem] * CHIPS,
        scratch_shapes=[pltpu.VMEM((16, C), F32)],
        compiler_params=pltpu.CompilerParams(vmem_limit_bytes=24 * 2**20),
        name="pieces",
    )(place, raw, decay, beta)


def head_kernel(
    place, scale_log, bias, mine, theirs, taps, gain, out, raw, decay, beta, local_out, reads, transit, adds
):
    z, core = place[0], place[1]
    head = 2 * z + core

    raw[:, 0:8] = jnp.zeros((3, 8, DK), F32)
    for distance in range(CHIPS):
        chip = lax.rem(z - distance + CHIPS, CHIPS)
        for source, its_core in ((mine, core), (theirs, 1 - core)):
            segment = 2 * chip + its_core
            to = pl.ds(pl.multiple_of(8 + segment * C, 8), C)
            raw[0, to] = source[distance, 0:C].astype(F32)
            raw[1, to] = source[distance, C : 2 * C].astype(F32)
            values = pl.ds(pl.multiple_of(2 * C + core * C, C), C)
            raw[2, to] = source[distance, values].astype(F32)
            rows = source[distance, CODES:PIECE].astype(F32)
            for first, codes in ((0, decay), (4, beta)):
                high = jnp.where(core == 0, rows[first : first + 1], rows[first + 1 : first + 2])
                low = jnp.where(core == 0, rows[first + 2 : first + 3], rows[first + 3 : first + 4])
                codes[pl.ds(segment, 1), :] = 16.0 * high + low

    level = decay[...] / 32.0 - 16.0 + bias[head]
    small = jnp.exp(-jnp.abs(level))
    one_more = 1.0 + small
    gap = one_more - 1.0
    log1p = jnp.where(gap == 0.0, small, jnp.log(one_more) * (small / jnp.where(gap == 0.0, 1.0, gap)))
    softplus = jnp.maximum(level, 0.0) + log1p
    log_decay = -jnp.exp(jnp.full((SEGMENTS, C), scale_log[head], F32)) * softplus
    row_ids = lax.broadcasted_iota(jnp.int32, (C, C), 0)
    col_ids = lax.broadcasted_iota(jnp.int32, (C, C), 1)
    sums = jnp.dot(
        log_decay,
        (row_ids <= col_ids).astype(F32),
        precision=lax.Precision.HIGHEST,
        preferred_element_type=F32,
    )
    strength = 1.0 / (1.0 + jnp.exp(8.0 - beta[...] / 32.0))
    start = jnp.exp(sums)
    end = jnp.exp(sums[:, C - 1 : C] - sums)
    columns = jnp.concatenate(
        [sums, strength, start, end, strength * start, jnp.zeros((C - 5 * SEGMENTS, C), F32)], 0
    ).T

    inclusive = row_ids >= col_ids
    strict = row_ids > col_ids

    def convolved(which, first, j):
        weights = taps[:, pl.ds(pl.multiple_of(first, DK), DK)]
        base = 8 + j * C - 3
        total = weights[0:1] * raw[which, base : base + C]
        for t in range(1, 4):
            total = total + weights[t : t + 1] * raw[which, base + t : base + t + C]
        return silu(total)

    for j in range(SEGMENTS):

        def column(kind):
            at = kind * SEGMENTS + j
            return columns[:, at : at + 1]

        queries = convolved(0, z * DK, j)
        keys = convolved(1, CHIPS * DK + z * DK, j)
        values = convolved(2, 2 * CHIPS * DK + head * DV, j)
        queries = queries * (
            lax.rsqrt(jnp.sum(queries * queries, -1, keepdims=True) + 1e-06) * (1.0 / math.sqrt(DK))
        )
        keys = keys * lax.rsqrt(jnp.sum(keys * keys, -1, keepdims=True) + 1e-06)
        qh, ql = split(queries)
        kh, kl = split(keys)
        pair = jnp.where(inclusive, jnp.exp(jnp.minimum(column(0) - sums[j : j + 1], 0.0)), 0.0)
        lower = jnp.where(strict, column(1) * pair * dot_t(kh, kh), 0.0)
        beyond = jnp.where((row_ids // 2 == col_ids // 2), -lower, 0.0)
        for b in (2, 4, 8, 16, 32, 64):
            part = jnp.where((row_ids // (2 * b) == col_ids // (2 * b)) & (row_ids // b != col_ids // b), lower, 0.0)
            near = beyond.astype(BF16)
            half = part + dot(part.astype(BF16), near)
            beyond = beyond - (half + dot(near, half.astype(BF16)))
        right = jnp.concatenate([column(1) * values, column(4) * keys], 1)
        solved = right + dot(beyond.astype(BF16), right.astype(BF16))
        gram = pair * (dot_t(jnp.concatenate([qh, ql], 1), jnp.concatenate([kh, kh], 1)) + dot_t(qh, kl))
        gh, gl = split(gram)
        new_values, write_keys = solved[:, :DV], solved[:, DV:]
        local_out[j] = dot3((gh, gl), split(new_values))
        read_high, read_low = split(column(2) * queries - dot(gh, write_keys.astype(BF16)))
        reads[j, :, :DK] = read_high
        reads[j, :, DK:] = read_low
        kh_t, kl_t = split(keys.T)
        transit[j] = dot(kh_t, (column(3) * write_keys).astype(BF16)).astype(BF16)
        adds[j] = dot3((kh_t, kl_t), split(column(3) * new_values))

    state = jnp.zeros((DK, DV), F32)
    for j in range(SEGMENTS):
        high, low = split(state)
        read = reads[j]
        rows = local_out[j] + dot(read, jnp.concatenate([high, high], 0)) + dot(read[:, :DK], low)
        square_mean = jnp.mean(rows * rows, -1, keepdims=True)
        out[j] = (rows * lax.rsqrt(square_mean + 1e-06) * gain[...]).astype(BF16)
        if j < SEGMENTS - 1:
            state = start[j : j + 1, C - 1 : C] * state - dot(transit[j], high) + adds[j]


def run_head(place, scale_log, bias, mine, theirs, taps, gain):
    vmem = pl.BlockSpec(memory_space=pltpu.VMEM)
    smem = pl.BlockSpec(memory_space=pltpu.SMEM)
    return pl.pallas_call(
        head_kernel,
        out_shape=jax.ShapeDtypeStruct((SEGMENTS, C, DV), BF16),
        in_specs=[smem, smem, smem, vmem, vmem, vmem, vmem],
        out_specs=vmem,
        scratch_shapes=[
            pltpu.VMEM((3, 8 + SEGMENTS * C, DK), F32),
            pltpu.VMEM((SEGMENTS, C), F32),
            pltpu.VMEM((SEGMENTS, C), F32),
            pltpu.VMEM((SEGMENTS, C, DV), F32),
            pltpu.VMEM((SEGMENTS, C, 2 * DK), BF16),
            pltpu.VMEM((SEGMENTS, DK, DK), BF16),
            pltpu.VMEM((SEGMENTS, DK, DV), F32),
        ],
        compiler_params=pltpu.CompilerParams(vmem_limit_bytes=40 * 2**20),
        name="head",
    )(place, scale_log, bias, mine, theirs, taps, gain)


def first_half_kernel(heads, gate, weight, normed, out):
    for h in range(VH):
        at = slice(h * DV, (h + 1) * DV)
        normed[:, at] = (heads[h].astype(F32) * silu(gate[:, at].astype(F32))).astype(BF16)
    out[...] = dot(normed[...], weight[...]).astype(BF16)


def second_half_kernel(place, normed, weight, first, out):
    core = place[1]
    out[:, pl.ds(pl.multiple_of(core * HALF, HALF), HALF)] = first[...]
    out[:, pl.ds(pl.multiple_of((1 - core) * HALF, HALF), HALF)] = dot(
        normed[...], weight[...]
    ).astype(BF16)


def project(place, heads, gate, weight, other_weight):
    vmem = pl.BlockSpec(memory_space=pltpu.VMEM)
    params = pltpu.CompilerParams(vmem_limit_bytes=32 * 2**20)
    normed, first = pl.pallas_call(
        first_half_kernel,
        out_shape=[jax.ShapeDtypeStruct((C, WIDTH), BF16), jax.ShapeDtypeStruct((C, HALF), BF16)],
        in_specs=[vmem] * 3,
        out_specs=[vmem] * 2,
        compiler_params=params,
        cost_estimate=pl.CostEstimate(flops=2 * C * WIDTH * HALF, bytes_accessed=2**23, transcendentals=0),
        name="project_first",
    )(heads, gate, weight)
    return pl.pallas_call(
        second_half_kernel,
        out_shape=jax.ShapeDtypeStruct((C, WIDTH), BF16),
        in_specs=[pl.BlockSpec(memory_space=pltpu.SMEM)] + [vmem] * 3,
        out_specs=vmem,
        compiler_params=params,
        cost_estimate=pl.CostEstimate(flops=2 * C * WIDTH * HALF, bytes_accessed=2**23, transcendentals=0),
        name="project_second",
    )(place, normed, other_weight, first)


def local(
    qkv_raw,
    output_gate,
    decay_codes,
    beta_codes,
    conv_weight,
    decay_scale_log,
    decay_bias,
    norm_gain,
    out_weight,
):
    index = lax.axis_index("seq")
    core = index % 2
    place = jnp.stack([index // 2, core]).astype(jnp.int32)
    columns = lax.dynamic_slice(out_weight, (0, core * HALF), (out_weight.shape[0], HALF))
    weight = lax.all_gather(columns, "fsdp", axis=0, tiled=True)

    pieces = cut_pieces(place, qkv_raw[0], decay_codes[0], beta_codes[0])
    arrived = {0: pieces[0]}
    for distance in (1, 7, 2, 6, 3, 5, 4):
        arrived[distance] = to_chip(pieces[distance], distance)
    mine = jnp.stack([arrived[distance] for distance in range(CHIPS)])
    theirs = other_core(mine)
    rows = run_head(place, decay_scale_log, decay_bias, mine, theirs, conv_weight, norm_gain[None])
    heads = lax.all_to_all(rows, "seq", 0, 0)
    heads, weight = lax.optimization_barrier((heads, weight))
    return project(place, heads, output_gate[0], weight, other_core(weight))[None]


def solution(mesh):
    return jax.shard_map(
        local,
        mesh=mesh,
        in_specs=(
            P("fsdp", "seq", None),
            P("fsdp", "seq", None),
            P("fsdp", None, "seq"),
            P("fsdp", None, "seq"),
            P(),
            P(),
            P(),
            P(),
            P("fsdp", None),
        ),
        out_specs=P("fsdp", "seq", None),
        check_vma=False,
    )
```

```python
import functools
import math

import jax
import jax.numpy as jnp
from jax import lax
from jax.experimental import pallas as pl
from jax.experimental.pallas import tpu as pltpu
from jax.sharding import PartitionSpec as P


CHIPS = 8
SEGMENTS = 16
C = 128
DK = 128
DV = 128
VH = 16
GROUP = 8
WIDTH = 2048
HALF = 1024
SIDE = 4
CODES = 4 * C
PIECE = CODES + 16
F32 = jnp.float32
BF16 = jnp.bfloat16


def to_chip(block, distance):
    return lax.ppermute(
        block, "seq", [(i, (i + 2 * distance) % SEGMENTS) for i in range(SEGMENTS)]
    )


def other_core(block):
    return lax.ppermute(block, "seq", [(i, i ^ 1) for i in range(SEGMENTS)])


def dot(left, right):
    return jnp.dot(left, right, preferred_element_type=F32)


def dot_t(left, right):
    return lax.dot_general(
        left, right, (((1,), (1,)), ((), ())), preferred_element_type=F32
    )


def split(value):
    high = value.astype(BF16)
    return high, (value - high.astype(F32)).astype(BF16)


def dot3(left, right):
    lh, ll = left
    rh, rl = right
    return dot(jnp.concatenate([lh, ll], 1), jnp.concatenate([rh, rh], 0)) + dot(lh, rl)


def silu(value):
    return value / (1.0 + jnp.exp(-value))


def pieces_kernel(place, raw, decay, beta, weight, *rest):
    outs, half, rows, decays, betas, sems = rest[:CHIPS], *rest[CHIPS:]
    z, core = place[0], place[1]
    copies = []

    def copy(source, target):
        copies.append(pltpu.make_async_copy(source, target, sems.at[len(copies)]))
        copies[-1].start()

    copy(decay, decays)
    copy(beta, betas)
    for distance in range(CHIPS):
        chip = lax.rem(z + distance, CHIPS)
        at = pl.multiple_of(chip * DK, DK)
        to = pl.multiple_of(chip * 2 * DV + 2 * CHIPS * DK, 2 * DV)
        for i, column in enumerate((at, at + CHIPS * DK, to, to + DV)):
            copy(raw.at[:, pl.ds(pl.multiple_of(column, DK), DK)], outs[distance].at[i * C : (i + 1) * C])
    copy(weight.at[:, pl.ds(pl.multiple_of(core * HALF, HALF), HALF)], half)
    copies[0].wait()
    copies[1].wait()
    rows[...] = jnp.zeros_like(rows)
    for distance in range(CHIPS):
        chip = lax.rem(z + distance, CHIPS)
        for first, codes in ((0, decays), (4, betas)):
            pair = codes[pl.ds(2 * chip, 2), :]
            rows[distance, first : first + 2] = (pair >> 4).astype(F32)
            rows[distance, first + 2 : first + 4] = (pair & 15).astype(F32)
        outs[distance][CODES:PIECE] = rows[distance].astype(BF16)
    for one in copies[2:]:
        one.wait()


def cut_pieces(place, raw, decay, beta, weight):
    vmem = pl.BlockSpec(memory_space=pltpu.VMEM)
    hbm = pl.BlockSpec(memory_space=pl.ANY)
    *pieces, half = pl.pallas_call(
        pieces_kernel,
        out_shape=[jax.ShapeDtypeStruct((PIECE, DK), BF16)] * CHIPS
        + [jax.ShapeDtypeStruct((weight.shape[0], HALF), BF16)],
        in_specs=[pl.BlockSpec(memory_space=pltpu.SMEM)] + [hbm] * 4,
        out_specs=[vmem] * (CHIPS + 1),
        scratch_shapes=[
            pltpu.VMEM((CHIPS, 16, C), F32),
            pltpu.VMEM((VH, C), jnp.int32),
            pltpu.VMEM((VH, C), jnp.int32),
            pltpu.SemaphoreType.DMA((3 + 4 * CHIPS,)),
        ],
        compiler_params=pltpu.CompilerParams(vmem_limit_bytes=60 * 2**20),
        name="pieces",
    )(place, raw, decay, beta, weight)
    return pieces, half


def head_kernel(
    place, scale_log, bias, mine, theirs, taps, gain, out, raw, decay, beta, local_out, reads, transit, adds,
    joins, grams, started, keys_t, rights,
):
    z, core = place[0], place[1]
    head = 2 * z + core

    raw[:, 0:8] = jnp.zeros((3, 8, DK), F32)
    for distance in range(CHIPS):
        chip = lax.rem(z - distance + CHIPS, CHIPS)
        for source, its_core in ((mine, core), (theirs, 1 - core)):
            segment = 2 * chip + its_core
            to = pl.ds(pl.multiple_of(8 + segment * C, 8), C)
            raw[0, to] = source[distance, 0:C].astype(F32)
            raw[1, to] = source[distance, C : 2 * C].astype(F32)
            values = pl.ds(pl.multiple_of(2 * C + core * C, C), C)
            raw[2, to] = source[distance, values].astype(F32)
            rows = source[distance, CODES:PIECE].astype(F32)
            for first, codes in ((0, decay), (4, beta)):
                high = jnp.where(core == 0, rows[first : first + 1], rows[first + 1 : first + 2])
                low = jnp.where(core == 0, rows[first + 2 : first + 3], rows[first + 3 : first + 4])
                codes[pl.ds(segment, 1), :] = 16.0 * high + low

    level = decay[...] / 32.0 - 16.0 + bias[head]
    small = jnp.exp(-jnp.abs(level))
    one_more = 1.0 + small
    gap = one_more - 1.0
    log1p = jnp.where(gap == 0.0, small, jnp.log(one_more) * (small / jnp.where(gap == 0.0, 1.0, gap)))
    softplus = jnp.maximum(level, 0.0) + log1p
    log_decay = -jnp.exp(jnp.full((SEGMENTS, C), scale_log[head], F32)) * softplus
    row_ids = lax.broadcasted_iota(jnp.int32, (C, C), 0)
    col_ids = lax.broadcasted_iota(jnp.int32, (C, C), 1)
    sums = jnp.dot(
        log_decay,
        (row_ids <= col_ids).astype(F32),
        precision=lax.Precision.HIGHEST,
        preferred_element_type=F32,
    )
    strength = 1.0 / (1.0 + jnp.exp(8.0 - beta[...] / 32.0))
    start = jnp.exp(sums)
    end = jnp.exp(sums[:, C - 1 : C] - sums)
    columns = jnp.concatenate(
        [sums, strength, start, end, strength * start, jnp.zeros((C - 5 * SEGMENTS, C), F32)], 0
    ).T

    inclusive = row_ids >= col_ids
    strict = row_ids > col_ids
    unit = (row_ids == col_ids).astype(BF16)

    def convolved(which, first, j):
        weights = taps[:, pl.ds(pl.multiple_of(first, DK), DK)]
        base = 8 + j * C - 3
        total = weights[0:1] * raw[which, base : base + C]
        for t in range(1, 4):
            total = total + weights[t : t + 1] * raw[which, base + t : base + t + C]
        return silu(total)

    def column(kind, j):
        at = kind * SEGMENTS + j
        return columns[:, at : at + 1]

    for level in range(1, 7):
        joins[level - 1] = (
            ((row_ids >> (level + 1)) == (col_ids >> (level + 1))) & ((row_ids >> level) != (col_ids >> level))
        ).astype(F32).astype(BF16)
    near = (row_ids >> 1) == (col_ids >> 1)

    states = [jnp.zeros((DK, DV), F32)]

    def chain(j):
        state = states[-1]
        high, low = split(state)
        if j < SEGMENTS - 1:
            states.append(start[j : j + 1, C - 1 : C] * state - dot(transit[j], high) + adds[j])
        read = reads[j]
        rows = local_out[j] + dot(read, jnp.concatenate([high, high], 0)) + dot(read[:, :DK], low)
        square_mean = jnp.mean(rows * rows, -1, keepdims=True)
        out[j] = (rows * lax.rsqrt(square_mean + 1e-06) * gain[...]).astype(BF16)

    waiting = []
    for group in range(0, SEGMENTS, GROUP):
        blocks = range(group, group + GROUP)
        kinv, right, qk, pairs = [], [], [], []
        lowers = []
        for i, j in enumerate(blocks):
            keys = convolved(1, CHIPS * DK + z * DK, j)
            keys = keys * lax.rsqrt(jnp.sum(keys * keys, -1, keepdims=True) + 1e-06)
            kh, kl = split(keys)
            pair = jnp.where(inclusive, jnp.exp(jnp.minimum(column(0, j) - sums[j : j + 1], 0.0)), 0.0)
            lower = jnp.where(strict, column(1, j) * pair * dot_t(kh, kh), 0.0)
            inverse = unit - jnp.where(near, lower, 0.0).astype(BF16)
            lowers.append(lower.astype(BF16))
            kinv.append(inverse)
            queries = convolved(0, z * DK, j)
            queries = queries * (
                lax.rsqrt(jnp.sum(queries * queries, -1, keepdims=True) + 1e-06) * (1.0 / math.sqrt(DK))
            )
            qh, ql = split(queries)
            gram = pair * (dot_t(jnp.concatenate([qh, ql], 1), jnp.concatenate([kh, kh], 1)) + dot_t(qh, kl))
            gh, gl = split(gram)
            grams[i, :, :C] = gh
            grams[i, :, C:] = gl
            started[i] = column(2, j) * queries
            kh_t, kl_t = split(keys.T)
            keys_t[i, :, :C] = kh_t
            keys_t[i, :, C:] = kl_t
            rights[i, :, DV:] = column(4, j) * keys
            rights[i, :, :DV] = column(1, j) * convolved(2, 2 * CHIPS * DK + head * DV, j)
        for level in range(6):
            half = [dot(lowers[i] * joins[level], kinv[i]).astype(BF16) for i in range(GROUP)]
            kinv = [kinv[i] - dot(kinv[i], half[i]).astype(BF16) for i in range(GROUP)]
            if waiting:
                waiting.pop(0)()
        solved = [rights[i] + dot(kinv[i] - unit, rights[i].astype(BF16)) for i in range(GROUP)]
        while waiting:
            waiting.pop(0)()
        for i, j in enumerate(blocks):
            new_values, write_keys = solved[i][:, :DV], solved[i][:, DV:]
            gh, gl = grams[i, :, :C], grams[i, :, C:]
            kh_t, kl_t = keys_t[i, :, :C], keys_t[i, :, C:]
            transit[j] = dot(kh_t, (column(3, j) * write_keys).astype(BF16)).astype(BF16)
            adds[j] = dot3((kh_t, kl_t), split(column(3, j) * new_values))
            local_out[j] = dot3((gh, gl), split(new_values))
            read_high, read_low = split(started[i] - dot(gh, write_keys.astype(BF16)))
            reads[j, :, :DK] = read_high
            reads[j, :, DK:] = read_low
            waiting.append(functools.partial(chain, j))
    while waiting:
        waiting.pop(0)()


def run_head(place, scale_log, bias, mine, theirs, taps, gain):
    vmem = pl.BlockSpec(memory_space=pltpu.VMEM)
    smem = pl.BlockSpec(memory_space=pltpu.SMEM)
    return pl.pallas_call(
        head_kernel,
        out_shape=jax.ShapeDtypeStruct((SEGMENTS, C, DV), BF16),
        in_specs=[smem, smem, smem, vmem, vmem, vmem, vmem],
        out_specs=vmem,
        scratch_shapes=[
            pltpu.VMEM((3, 8 + SEGMENTS * C, DK), F32),
            pltpu.VMEM((SEGMENTS, C), F32),
            pltpu.VMEM((SEGMENTS, C), F32),
            pltpu.VMEM((SEGMENTS, C, DV), F32),
            pltpu.VMEM((SEGMENTS, C, 2 * DK), BF16),
            pltpu.VMEM((SEGMENTS, DK, DK), BF16),
            pltpu.VMEM((SEGMENTS, DK, DV), F32),
            pltpu.VMEM((6, C, C), BF16),
            pltpu.VMEM((GROUP, C, 2 * C), BF16),
            pltpu.VMEM((GROUP, C, DK), F32),
            pltpu.VMEM((GROUP, DK, 2 * C), BF16),
            pltpu.VMEM((GROUP, C, DV + DK), F32),
        ],
        compiler_params=pltpu.CompilerParams(vmem_limit_bytes=40 * 2**20),
        cost_estimate=pl.CostEstimate(flops=10**10, bytes_accessed=2**25, transcendentals=0),
        name="head",
    )(place, scale_log, bias, mine, theirs, taps, gain)


def in_order_of(place, core, heads, ordered):
    y, x = place[2], place[3]
    for second in range(SIDE):
        for first in range(SIDE):
            back_x = jnp.where(core == 0, first, second)
            back_y = jnp.where(core == 0, second, first)
            head = lax.rem(y - back_y + SIDE, SIDE) * SIDE + lax.rem(x - back_x + SIDE, SIDE)
            at = (second * SIDE + first) * DV
            ordered[:, at : at + DV] = heads[head]


def product_of(ordered, weights):
    width = SIDE * DV
    total = dot(ordered[:, :width], weights[0][...].reshape(width, HALF))
    for second in range(1, SIDE):
        at = second * width
        total = total + dot(ordered[:, at : at + width], weights[second][...].reshape(width, HALF))
    return total.astype(BF16)


def project_kernel(place, heads, gate, *rest):
    own, others, out, normed, ordered = rest[:SIDE], rest[SIDE : 2 * SIDE], *rest[2 * SIDE :]
    core = place[1]
    for h in range(VH):
        at = slice(h * DV, (h + 1) * DV)
        normed[h] = (heads[h].astype(F32) * silu(gate[:, at].astype(F32))).astype(BF16)
    for its_core, weights in ((core, own), (1 - core, others)):
        in_order_of(place, its_core, normed, ordered)
        out[:, pl.ds(pl.multiple_of(its_core * HALF, HALF), HALF)] = product_of(ordered, weights)


def project(place, heads, gate, weights, other_weights):
    vmem = pl.BlockSpec(memory_space=pltpu.VMEM)
    return pl.pallas_call(
        project_kernel,
        out_shape=jax.ShapeDtypeStruct((C, WIDTH), BF16),
        in_specs=[pl.BlockSpec(memory_space=pltpu.SMEM)] + [vmem] * (2 + 2 * SIDE),
        out_specs=vmem,
        compiler_params=pltpu.CompilerParams(vmem_limit_bytes=40 * 2**20),
        cost_estimate=pl.CostEstimate(flops=2 * C * WIDTH * WIDTH, bytes_accessed=2**23, transcendentals=0),
        scratch_shapes=[pltpu.VMEM((VH, C, DV), BF16), pltpu.VMEM((C, WIDTH), BF16)],
        name="project",
    )(place, heads, gate, *weights, *other_weights)


def along(block, distance, second):
    route = []
    for i in range(SEGMENTS):
        by_x = (i % 2 == 0) != second
        for y in range(SIDE):
            for x in range(SIDE):
                to_y, to_x = (y, (x + distance) % SIDE) if by_x else ((y + distance) % SIDE, x)
                route.append(((i * SIDE + y) * SIDE + x, (i * SIDE + to_y) * SIDE + to_x))
    return lax.ppermute(block, ("seq", "fsdp"), route)


def local(
    qkv_raw,
    output_gate,
    decay_codes,
    beta_codes,
    conv_weight,
    decay_scale_log,
    decay_bias,
    norm_gain,
    out_weight,
):
    index, row = lax.axis_index("seq"), lax.axis_index("fsdp")
    place = jnp.stack([index // 2, index % 2, row // SIDE, row % SIDE]).astype(jnp.int32)
    barrier = lax.optimization_barrier

    pieces, half = cut_pieces(place, qkv_raw[0], decay_codes[0], beta_codes[0], out_weight)
    arrived = {0: pieces[0]}
    for distance in (1, 7, 2, 6, 3, 5, 4):
        arrived[distance] = to_chip(pieces[distance], distance)
    half, arrived[2], arrived[6] = barrier((half, arrived[2], arrived[6]))
    line = jnp.stack([half] + [along(half, distance, False) for distance in (1, 2, 3)])
    mine = jnp.stack([arrived[distance] for distance in range(CHIPS)])
    mine, line = barrier((mine, line))
    theirs, other_line = other_core(mine), other_core(line)
    weights = [line] + [along(line, distance, True) for distance in (1, 2, 3)]
    rows = run_head(place, decay_scale_log, decay_bias, mine, theirs, conv_weight, norm_gain[None])
    heads = lax.all_to_all(rows, "seq", 0, 0)
    heads, *later = barrier((heads, *weights[1:]))
    weights = [line, *later]
    other_weights = [other_line] + [other_core(weight) for weight in later]
    return project(place, heads, output_gate[0], weights, other_weights)[None]


def solution(mesh):
    return jax.shard_map(
        local,
        mesh=mesh,
        in_specs=(
            P("fsdp", "seq", None),
            P("fsdp", "seq", None),
            P("fsdp", None, "seq"),
            P("fsdp", None, "seq"),
            P(),
            P(),
            P(),
            P(),
            P("fsdp", None),
        ),
        out_specs=P("fsdp", "seq", None),
        check_vma=False,
    )
```

```python
import math

import jax
import jax.numpy as jnp
from jax import lax
from jax.experimental import pallas as pl
from jax.experimental.pallas import tpu as pltpu
from jax.sharding import PartitionSpec as P


CHIPS = 8
SEGMENTS = 16
C = 128
DK = 128
DV = 128
VH = 16
HEADS = 8
KEYS = 4
BLOCKS = 2
WIDTH = 2048
HALF = 1024
QK = KEYS * DK
RAW = 2 * QK + HEADS * DV
ROW = RAW + HEADS * DV
TALL = C + 16
TERMS_MIB = 60
SIDE = 4
F32 = jnp.float32
BF16 = jnp.bfloat16
VMEM = pl.BlockSpec(memory_space=pltpu.VMEM)
SMEM = pl.BlockSpec(memory_space=pltpu.SMEM)


def to_chip(block, distance):
    return lax.ppermute(
        block, "seq", [(i, (i + 2 * distance) % SEGMENTS) for i in range(SEGMENTS)]
    )


def other_core(block):
    return lax.ppermute(block, "seq", [(i, i ^ 1) for i in range(SEGMENTS)])


def between_chips(blocks):
    groups = [[2 * z + c for z in range(CHIPS)] for c in range(2)]
    return lax.all_to_all(blocks, "seq", 0, 0, axis_index_groups=groups)


def dot(left, right):
    return jnp.dot(left, right, preferred_element_type=F32)


def dot_t(left, right):
    return lax.dot_general(
        left, right, (((1,), (1,)), ((), ())), preferred_element_type=F32
    )


def split(value):
    high = value.astype(BF16)
    return high, (value - high.astype(F32)).astype(BF16)


def dot3(left, right):
    lh, ll = left
    rh, rl = right
    return dot(jnp.concatenate([lh, ll], 1), jnp.concatenate([rh, rh], 0)) + dot(lh, rl)


def silu(value):
    return value / (1.0 + jnp.exp(-value))


ANY = pl.BlockSpec(memory_space=pl.ANY)
KEPT = (
    ((C, C), F32),
    ((BLOCKS * HEADS, C), F32),
    ((BLOCKS * HEADS, C, C), F32),
    ((BLOCKS * KEYS, C, 2 * DK), BF16),
    ((BLOCKS * HEADS, C, 2 * DV + 2 * DK), BF16),
    ((HEADS, DK, DK), BF16),
    ((HEADS, DK, 2 * DV), BF16),
)


def shape(dims, kind):
    return jax.ShapeDtypeStruct(dims, kind)


def my_core():
    return lax.rem(lax.axis_index("seq"), 2)


def params(mib):
    return pltpu.CompilerParams(vmem_limit_bytes=mib * 2**20)


def cost(flops, moved):
    return pl.CostEstimate(flops=flops, bytes_accessed=moved, transcendentals=0)


def cut_kernel(raw, gate, decay, beta, weight, give, tail, half, rows, decays, betas, sems):
    core = my_core()
    copies = []

    def copy(source, target):
        copies.append(pltpu.make_async_copy(source, target, sems.at[len(copies)]))
        copies[-1].start()

    def cut(ref, first, width, part, at=0, count=C):
        column = pl.multiple_of(first + part * width, width)
        return ref.at[at : at + count, pl.ds(column, width)]

    copy(decay, decays)
    copy(beta, betas)
    parts = ((0, QK, 0), (2 * QK, QK, QK), (4 * QK, HEADS * DV, 2 * QK))
    for first, width, to in parts:
        copy(cut(raw, first, width, 1 - core), give.at[0:C, to : to + width])
    copy(cut(gate, 0, HEADS * DV, 1 - core), give.at[0:C, RAW:ROW])
    for first, width, to in parts:
        copy(cut(raw, first, width, core, C - 16, 16), tail.at[:, to : to + width])
    copy(cut(weight, 0, HALF, core), half)
    give[C:TALL, 2 * C :] = jnp.zeros((16, ROW - 2 * C), BF16)
    copies[0].wait()
    copies[1].wait()
    for at, codes in ((0, decays), (C, betas)):
        code = codes[pl.ds(pl.multiple_of((1 - core) * HEADS, HEADS), HEADS), :]
        rows[0:HEADS, at : at + C] = (code >> 4).astype(F32)
        rows[HEADS:16, at : at + C] = (code & 15).astype(F32)
    give[C:TALL, 0 : 2 * C] = rows[...].astype(BF16)
    for one in copies[2:]:
        one.wait()


def cut_rows(raw, gate, decay, beta, weight):
    return pl.pallas_call(
        cut_kernel,
        out_shape=[
            shape((TALL, ROW), BF16),
            shape((16, RAW), BF16),
            shape((weight.shape[0], HALF), BF16),
        ],
        in_specs=[ANY] * 5,
        out_specs=[VMEM] * 3,
        scratch_shapes=[
            pltpu.VMEM((16, 2 * C), F32),
            pltpu.VMEM((VH, C), jnp.int32),
            pltpu.VMEM((VH, C), jnp.int32),
            pltpu.SemaphoreType.DMA((10,)),
        ],
        compiler_params=params(60),
        name="cut",
    )(raw, gate, decay, beta, weight)


def assemble(core, staged, halo, raw, first, width):
    at = slice(first, first + width)
    raw[0:8] = halo[:, at].astype(F32)[8:16]
    for i, block in enumerate((core, 1 - core)):
        raw[pl.ds(pl.multiple_of(8 + block * C, 8), C)] = staged[i].astype(F32)


def convolved(raw, taps, at, channel, j):
    weights = taps[:, pl.ds(pl.multiple_of(channel, DK), DK)]
    base = 8 + j * C - 3
    total = weights[0:1] * raw[base : base + C, at : at + DK]
    for t in range(1, 4):
        total = total + weights[t : t + 1] * raw[base + t : base + t + C, at : at + DK]
    return silu(total)


def over_length(value):
    return lax.rsqrt(jnp.sum(value * value, -1, keepdims=True) + 1e-06)


def unit_of(j, h):
    return j * HEADS + h


def column(columns, kind, unit):
    at = kind * BLOCKS * HEADS + unit
    return columns[:, at : at + 1]


def terms_kernel(
    scale_log, bias, decay_codes, beta_codes, own, got, halo, taps,
    message, *rest,
):
    outs, kept, rest = rest[: len(KEPT)], rest[len(KEPT) : 2 * len(KEPT)], rest[2 * len(KEPT) :]
    raw, staged, their_codes, decay, beta, joins, keys_t, rights, transit, arrive, sems = rest
    columns, starts, pairs, keys_out, solved_out, early_transit, early_add = kept
    core = my_core()
    copies = []
    column_of = pl.multiple_of(2 * QK + core * QK, QK), pl.multiple_of(4 * QK + core * HEADS * DV, HEADS * DV)
    loads = [
        pltpu.make_async_copy(*one, arrive.at[i])
        for i, one in enumerate((
            (own.at[:, pl.ds(column_of[0], QK)], staged.at[0, :, 0:QK]),
            (own.at[:, pl.ds(column_of[1], HEADS * DV)], staged.at[0, :, QK:]),
            (got.at[0:C, QK:RAW], staged.at[1]),
            (got.at[C:TALL, 0 : 2 * C], their_codes),
        ))
    ]
    for one in loads:
        one.start()

    def leave(which, first=0, count=None):
        source, target = kept[which], outs[which]
        if count:
            source, target = source.at[first : first + count], target.at[first : first + count]
        copies.append(pltpu.make_async_copy(source, target, sems.at[len(copies)]))
        copies[-1].start()

    loads[3].wait()
    codes = their_codes[...].astype(F32)
    ours = pl.ds(pl.multiple_of(core * HEADS, HEADS), HEADS)
    theirs = pl.ds(pl.multiple_of((1 - core) * HEADS, HEADS), HEADS)
    decay[ours, :] = decay_codes[ours, :].astype(F32)
    beta[ours, :] = beta_codes[ours, :].astype(F32)
    decay[theirs, :] = 16.0 * codes[0:HEADS, 0:C] + codes[HEADS:16, 0:C]
    beta[theirs, :] = 16.0 * codes[0:HEADS, C:] + codes[HEADS:16, C:]

    def by_head(ref):
        rows = [jnp.full((1, C), ref[core * HEADS + h], F32) for h in range(HEADS)]
        return jnp.concatenate(rows * BLOCKS, 0)

    level = decay[...] / 32.0 - 16.0 + by_head(bias)
    small = jnp.exp(-jnp.abs(level))
    one_more = 1.0 + small
    gap = one_more - 1.0
    log1p = jnp.where(gap == 0.0, small, jnp.log(one_more) * (small / jnp.where(gap == 0.0, 1.0, gap)))
    log_decay = -jnp.exp(by_head(scale_log)) * (jnp.maximum(level, 0.0) + log1p)
    row_ids = lax.broadcasted_iota(jnp.int32, (C, C), 0)
    col_ids = lax.broadcasted_iota(jnp.int32, (C, C), 1)
    sums = jnp.dot(
        log_decay,
        (row_ids <= col_ids).astype(F32),
        precision=lax.Precision.HIGHEST,
        preferred_element_type=F32,
    )
    strength = 1.0 / (1.0 + jnp.exp(8.0 - beta[...] / 32.0))
    start = jnp.exp(sums)
    starts[...] = start
    end = jnp.exp(sums[:, C - 1 : C] - sums)
    units = BLOCKS * HEADS
    columns[...] = jnp.concatenate(
        [sums, strength, start, end, strength * start, jnp.zeros((C - 5 * units, C), F32)], 0
    ).T

    leave(0)
    leave(1)
    inclusive = row_ids >= col_ids
    strict = row_ids > col_ids
    eye = (row_ids == col_ids).astype(BF16)
    for k in range(1, 7):
        joins[k - 1] = (
            ((row_ids >> (k + 1)) == (col_ids >> (k + 1))) & ((row_ids >> k) != (col_ids >> k))
        ).astype(F32).astype(BF16)
    near = (row_ids >> 1) == (col_ids >> 1)

    for one in loads[:3]:
        one.wait()
    assemble(core, staged, halo, raw, QK, RAW - QK)
    for j in range(BLOCKS):
        lowers, inverses = [], []
        for g in range(KEYS):
            keys = convolved(raw, taps, g * DK, 2 * QK + core * QK + g * DK, j)
            keys = keys * over_length(keys)
            kh, kl = split(keys)
            keys_out[j * KEYS + g, :, :DK] = kh
            keys_out[j * KEYS + g, :, DK:] = kl
            kh_t, kl_t = split(keys.T)
            keys_t[g, :, :C] = kh_t
            keys_t[g, :, C:] = kl_t
            gram = dot_t(kh, kh)
            for h in (2 * g, 2 * g + 1):
                u = unit_of(j, h)
                pair = jnp.where(inclusive, jnp.exp(jnp.minimum(column(columns, 0, u) - sums[u : u + 1], 0.0)), 0.0)
                pairs[u] = pair
                lower = jnp.where(strict, column(columns, 1, u) * pair * gram, 0.0)
                lowers.append(lower.astype(BF16))
                inverses.append(eye - jnp.where(near, lower, 0.0).astype(BF16))
                values = convolved(raw, taps, QK + h * DV, 4 * QK + core * HEADS * DV + h * DV, j)
                rights[h, :, :DV] = column(columns, 1, u) * values
                rights[h, :, DV:] = column(columns, 4, u) * keys
        leave(2, j * HEADS, HEADS)
        leave(3, j * KEYS, KEYS)
        for k in range(6):
            halves = [dot(lowers[h] * joins[k], inverses[h]).astype(BF16) for h in range(HEADS)]
            inverses = [inverses[h] - dot(inverses[h], halves[h]).astype(BF16) for h in range(HEADS)]
        for h in range(HEADS):
            u = unit_of(j, h)
            solved = rights[h] + dot(inverses[h] - eye, rights[h].astype(BF16))
            values, writes = solved[:, :DV], solved[:, DV:]
            high, low = split(values)
            solved_out[u, :, :DV] = high
            solved_out[u, :, DV : 2 * DV] = low
            high, low = split(writes)
            solved_out[u, :, 2 * DV : 2 * DV + DK] = high
            solved_out[u, :, 2 * DV + DK :] = low
            leave(4, u, 1)
            kt = keys_t[h // 2, :, :C], keys_t[h // 2, :, C:]
            moved = dot3(kt, split(column(columns, 3, u) * writes))
            add = dot3(kt, split(column(columns, 3, u) * values))
            last = start[u : u + 1, C - 1 : C]
            if j == 0:
                transit[h] = moved
                early_transit[h] = moved.astype(BF16)
                add_high, add_low = split(add)
                early_add[h, :, :DV] = add_high
                early_add[h, :, DV:] = add_low
            else:
                first = start[unit_of(0, h) : unit_of(0, h) + 1, C - 1 : C]
                second = moved.astype(BF16)
                crossed = dot(second, jnp.concatenate([early_transit[h], early_add[h, :, :DV]], 1))
                earlier = early_add[h, :, :DV].astype(F32) + early_add[h, :, DV:].astype(F32)
                message[h, 0:C, :DK] = (last * transit[h] + first * moved - crossed[:, :DK]).astype(BF16)
                message[h, 0:C, DK:] = (last * earlier - crossed[:, DK:] + add).astype(BF16)
                both = jnp.broadcast_to(first * last, (1, DK))
                top = both.astype(BF16).astype(F32)
                middle = (both - top).astype(BF16).astype(F32)
                parts = jnp.concatenate([top, middle, both - top - middle, jnp.zeros((13, DK), F32)], 0)
                message[h, C:TALL, :DK] = parts.astype(BF16)
                message[h, C:TALL, DK:] = jnp.zeros((16, DV), BF16)
        if j == 0:
            leave(5)
            leave(6)
    for one in copies:
        one.wait()


def run_terms(*operands):
    units = BLOCKS * HEADS
    return pl.pallas_call(
        terms_kernel,
        out_shape=[shape((HEADS, TALL, DK + DV), BF16)] + [shape(*one) for one in KEPT],
        in_specs=[SMEM] * 2 + [VMEM] * 2 + [ANY] * 2 + [VMEM] * 2,
        out_specs=[VMEM] + [ANY] * len(KEPT),
        scratch_shapes=[pltpu.VMEM(*one) for one in KEPT]
        + [
            pltpu.VMEM((8 + BLOCKS * C, RAW - QK), F32),
            pltpu.VMEM((BLOCKS, C, RAW - QK), BF16),
            pltpu.VMEM((16, 2 * C), BF16),
            pltpu.VMEM((units, C), F32),
            pltpu.VMEM((units, C), F32),
            pltpu.VMEM((6, C, C), BF16),
            pltpu.VMEM((KEYS, DK, 2 * C), BF16),
            pltpu.VMEM((HEADS, C, DV + DK), F32),
            pltpu.VMEM((HEADS, DK, DK), F32),
            pltpu.SemaphoreType.DMA((4,)),
            pltpu.SemaphoreType.DMA((24,)),
        ],
        compiler_params=params(TERMS_MIB),
        cost_estimate=cost(8 * 10**9, 2**25),
        name="terms",
    )(*operands)


def reads_kernel(own, got, halo, taps, *rest):
    sources, (base, reads), kept = rest[: len(KEPT)], rest[len(KEPT) : len(KEPT) + 2], rest[len(KEPT) + 2 : -5]
    bases, readers, raw, staged, sems = rest[-5:]
    core = my_core()
    columns, starts, pairs, keys, solved, early_transit, early_add = kept
    copies = []

    def move(source, target, first=None, count=HEADS):
        if first is not None:
            source, target = source.at[first : first + count], target.at[first : first + count]
        copies.append(pltpu.make_async_copy(source, target, sems.at[len(copies)]))
        copies[-1].start()

    move(own.at[:, pl.ds(pl.multiple_of(core * QK, QK), QK)], staged.at[0])
    move(got.at[0:C, 0:QK], staged.at[1])
    for i in (0, 1, 3):
        move(sources[i], kept[i])
    for j in range(BLOCKS):
        move(sources[2], pairs, j * HEADS)
        move(sources[4], solved, j * HEADS)
        if j == 0:
            move(sources[5], early_transit)
            move(sources[6], early_add)
    for one in copies[:5]:
        one.wait()
    assemble(core, staged, halo, raw, 0, QK)
    for j in range(BLOCKS):
        for one in copies[5:7] if j == 0 else copies[7:11]:
            one.wait()
        for g in range(KEYS):
            queries = convolved(raw, taps, g * DK, core * QK + g * DK, j)
            queries = queries * (over_length(queries) * (1.0 / math.sqrt(DK)))
            qh, ql = split(queries)
            both = keys[j * KEYS + g]
            kh, kl = both[:, :DK], both[:, DK:]
            plain = dot_t(jnp.concatenate([qh, ql], 1), jnp.concatenate([kh, kh], 1)) + dot_t(qh, kl)
            for h in (2 * g, 2 * g + 1):
                u = unit_of(j, h)
                gram = split(pairs[u] * plain)
                inner = solved[u]
                out = dot3(gram, (inner[:, :DV], inner[:, DV : 2 * DV]))
                writes = inner[:, 2 * DV : 2 * DV + DK], inner[:, 2 * DV + DK :]
                read = column(columns, 2, u) * queries - dot3(gram, writes)
                if j:
                    high, low = split(read)
                    out = out + dot3((high, low), (early_add[h, :, :DV], early_add[h, :, DV:]))
                    before = unit_of(0, h)
                    read = starts[before : before + 1, C - 1 : C] * read - dot(high, early_transit[h])
                bases[u] = out
                high, low = split(read)
                readers[u, :, :DK] = high
                readers[u, :, DK:] = low
        move(bases, base, j * HEADS)
        move(readers, reads, j * HEADS)
    for one in copies[11:]:
        one.wait()


def run_reads(*operands):
    units = BLOCKS * HEADS
    return pl.pallas_call(
        reads_kernel,
        out_shape=[shape((units, C, DV), F32), shape((units, C, 2 * DK), BF16)],
        in_specs=[ANY] * 2 + [VMEM] * 2 + [ANY] * len(KEPT),
        out_specs=[ANY] * 2,
        scratch_shapes=[pltpu.VMEM(*one) for one in KEPT]
        + [
            pltpu.VMEM((units, C, DV), F32),
            pltpu.VMEM((units, C, 2 * DK), BF16),
            pltpu.VMEM((8 + BLOCKS * C, QK), F32),
            pltpu.VMEM((BLOCKS, C, QK), BF16),
            pltpu.SemaphoreType.DMA((15,)),
        ],
        compiler_params=params(TERMS_MIB),
        cost_estimate=cost(4 * 10**9, 2**24),
        name="reads",
    )(*operands)


def enter_kernel(arrived, entering, messages, sems):
    copies = [
        pltpu.make_async_copy(arrived.at[chip], messages.at[chip], sems.at[chip]) for chip in range(CHIPS - 1)
    ]
    for one in copies:
        one.start()
    state = jnp.zeros((DK, DV), F32)
    for chip in range(CHIPS):
        high = state.astype(BF16)
        entering[chip] = high
        if chip < CHIPS - 1:
            copies[chip].wait()
            parts = messages[chip, C:TALL, :DK].astype(F32)
            factor = parts[0:1] + parts[1:2] + parts[2:3]
            state = factor * state - dot(messages[chip, 0:C, :DK], high) + messages[chip, 0:C, DK:].astype(F32)


def run_enter(messages):
    return pl.pallas_call(
        enter_kernel,
        out_shape=shape((CHIPS, DK, DV), BF16),
        in_specs=[ANY],
        out_specs=VMEM,
        scratch_shapes=[pltpu.VMEM((CHIPS, TALL, DK + DV), BF16), pltpu.SemaphoreType.DMA((CHIPS - 1,))],
        compiler_params=params(TERMS_MIB),
        cost_estimate=cost(10**9, 2**20),
        name="enter",
    )(messages)


def finish_kernel(arrived, base, reads, gate, got, gain, mine, theirs, entering, bases, readers, gates, sems):
    core = my_core()
    blocks = 1 - core, core
    loads = [pltpu.make_async_copy(arrived, entering, sems.at[6])]
    loads[0].start()
    for i, block in enumerate(blocks):
        units = pl.ds(pl.multiple_of(block * HEADS, HEADS), HEADS)
        column_of = pl.multiple_of(core * HEADS * DV, HEADS * DV)
        a_gate = gate.at[:, pl.ds(column_of, HEADS * DV)] if i else got.at[0:C, RAW:ROW]
        for source, target in ((a_gate, gates), (reads.at[units], readers), (base.at[units], bases)):
            loads.append(pltpu.make_async_copy(source, target.at[i], sems.at[len(loads) - 1]))
            loads[-1].start()
    for i, out in enumerate((theirs, mine)):
        for one in loads[4:] if i else loads[:4]:
            one.wait()
        for h in range(HEADS):
            state = entering[h]
            rows = bases[i, h] + dot(readers[i, h], jnp.concatenate([state, state], 0))
            square_mean = jnp.mean(rows * rows, -1, keepdims=True)
            opening = silu(gates[i, :, h * DV : (h + 1) * DV].astype(F32))
            out[h] = (rows * lax.rsqrt(square_mean + 1e-06) * gain[...] * opening).astype(BF16)


def run_finish(entering, base, reads, gate, got, gain):
    return pl.pallas_call(
        finish_kernel,
        out_shape=[shape((HEADS, C, DV), BF16)] * 2,
        in_specs=[ANY] * 5 + [VMEM],
        out_specs=[VMEM] * 2,
        scratch_shapes=[
            pltpu.VMEM((HEADS, DK, DV), BF16),
            pltpu.VMEM((BLOCKS, HEADS, C, DV), F32),
            pltpu.VMEM((BLOCKS, HEADS, C, 2 * DK), BF16),
            pltpu.VMEM((BLOCKS, C, HEADS * DV), BF16),
            pltpu.SemaphoreType.DMA((7,)),
        ],
        compiler_params=params(TERMS_MIB),
        cost_estimate=cost(2 * 10**9, 2**22),
        name="finish",
    )(entering, base, reads, gate, got, gain)


def in_order_of(core, heads, ordered):
    row = lax.axis_index("fsdp")
    y, x = row // SIDE, lax.rem(row, SIDE)
    for second in range(SIDE):
        for first in range(SIDE):
            back_x = jnp.where(core == 0, first, second)
            back_y = jnp.where(core == 0, second, first)
            head = lax.rem(y - back_y + SIDE, SIDE) * SIDE + lax.rem(x - back_x + SIDE, SIDE)
            at = (second * SIDE + first) * DV
            ordered[:, at : at + DV] = heads[head]


def product_of(ordered, weights):
    width = SIDE * DV
    total = dot(ordered[:, :width], weights[0][...].reshape(width, HALF))
    for second in range(1, SIDE):
        at = second * width
        total = total + dot(ordered[:, at : at + width], weights[second][...].reshape(width, HALF))
    return total.astype(BF16)


def first_kernel(mine, theirs, *rest):
    weights, (normed, out, ordered) = rest[:SIDE], rest[SIDE:]
    core = my_core()
    for source, its_core in ((mine, core), (theirs, 1 - core)):
        normed[pl.ds(its_core * HEADS, HEADS)] = source[...]
    in_order_of(core, normed, ordered)
    out[...] = product_of(ordered, weights)


def second_kernel(normed, first, *rest):
    weights, (out, ordered) = rest[:SIDE], rest[SIDE:]
    core = my_core()
    in_order_of(1 - core, normed, ordered)
    out[:, pl.ds(pl.multiple_of(core * HALF, HALF), HALF)] = first[...]
    out[:, pl.ds(pl.multiple_of((1 - core) * HALF, HALF), HALF)] = product_of(ordered, weights)


def project(mine, theirs, weights, other_weights):
    settings = dict(
        in_specs=[VMEM] * (2 + SIDE),
        compiler_params=params(40),
        cost_estimate=cost(C * WIDTH * WIDTH, 2**22),
        scratch_shapes=[pltpu.VMEM((C, WIDTH), BF16)],
    )
    normed, first = pl.pallas_call(
        first_kernel,
        out_shape=[shape((VH, C, DV), BF16), shape((C, HALF), BF16)],
        out_specs=[VMEM] * 2,
        name="project_first",
        **settings,
    )(mine, theirs, *weights)
    return pl.pallas_call(
        second_kernel,
        out_shape=shape((C, WIDTH), BF16),
        out_specs=VMEM,
        name="project_second",
        **settings,
    )(normed, first, *other_weights)


def along(block, distance, second):
    route = []
    for i in range(SEGMENTS):
        by_x = (i % 2 == 0) != second
        for y in range(SIDE):
            for x in range(SIDE):
                to_y, to_x = (y, (x + distance) % SIDE) if by_x else ((y + distance) % SIDE, x)
                route.append(((i * SIDE + y) * SIDE + x, (i * SIDE + to_y) * SIDE + to_x))
    return lax.ppermute(block, ("seq", "fsdp"), route)


def local(
    qkv_raw,
    output_gate,
    decay_codes,
    beta_codes,
    conv_weight,
    decay_scale_log,
    decay_bias,
    norm_gain,
    out_weight,
):
    barrier = lax.optimization_barrier
    raw, decay, beta = qkv_raw[0], decay_codes[0], beta_codes[0]
    give, tail, half = cut_rows(raw, output_gate[0], decay, beta, out_weight)
    got = other_core(give)
    tail = jnp.where(lax.axis_index("seq") % 2 == 0, got[C - 16 : C, :RAW], tail)
    halo = lax.ppermute(tail, "seq", [(i, i + 2) for i in range(SEGMENTS - 2)])
    parts = [along(half, distance, False) for distance in (1, 2, 3)]
    message, *kept = run_terms(
        decay_scale_log, decay_bias, decay, beta, raw, got, halo, conv_weight
    )
    message, half, *parts = barrier((message, half, *parts))
    messages = between_chips(message)
    line = jnp.stack([half, *parts])
    later = [along(line, distance, True) for distance in (1, 2, 3)]
    other_line = other_core(line)
    base, reads = run_reads(raw, got, halo, conv_weight, *kept)
    messages, base, reads = barrier((messages, base, reads))
    entering = between_chips(run_enter(messages))
    entering, *later = barrier((entering, *later))
    other_weights = [other_line] + [other_core(weight) for weight in later]
    mine, theirs = run_finish(entering, base, reads, output_gate[0], got, norm_gain[None])
    return project(mine, other_core(theirs), [line, *later], other_weights)[None]


def solution(mesh):
    return jax.shard_map(
        local,
        mesh=mesh,
        in_specs=(
            P("fsdp", "seq", None),
            P("fsdp", "seq", None),
            P("fsdp", None, "seq"),
            P("fsdp", None, "seq"),
            P(),
            P(),
            P(),
            P(),
            P("fsdp", None),
        ),
        out_specs=P("fsdp", "seq", None),
        check_vma=False,
    )
```

```python
import math

import jax
import jax.numpy as jnp
from jax import lax
from jax.experimental import pallas as pl
from jax.experimental.pallas import tpu as pltpu
from jax.sharding import PartitionSpec as P


CHIPS = 8
SEGMENTS = 16
C = 128
DK = 128
DV = 128
VH = 16
HEADS = 8
KEYS = 4
BLOCKS = 2
WIDTH = 2048
HALF = 1024
QK = KEYS * DK
RAW = 2 * QK + HEADS * DV
ROW = RAW + HEADS * DV
TALL = C + 16
TERMS_MIB = 60
WHOLE = 2 * DK + 16
SIDE = 4
F32 = jnp.float32
BF16 = jnp.bfloat16
VMEM = pl.BlockSpec(memory_space=pltpu.VMEM)
SMEM = pl.BlockSpec(memory_space=pltpu.SMEM)


def to_chip(block, distance):
    return lax.ppermute(
        block, "seq", [(i, (i + 2 * distance) % SEGMENTS) for i in range(SEGMENTS)]
    )


def other_core(block):
    return lax.ppermute(block, "seq", [(i, i ^ 1) for i in range(SEGMENTS)])


def between_chips(blocks):
    groups = [[2 * z + c for z in range(CHIPS)] for c in range(2)]
    return lax.all_to_all(blocks, "seq", 0, 0, axis_index_groups=groups)


def dot(left, right):
    return jnp.dot(left, right, preferred_element_type=F32)


def dot_t(left, right):
    return lax.dot_general(
        left, right, (((1,), (1,)), ((), ())), preferred_element_type=F32
    )


def split(value):
    high = value.astype(BF16)
    return high, (value - high.astype(F32)).astype(BF16)


def dot3(left, right):
    lh, ll = left
    rh, rl = right
    return dot(jnp.concatenate([lh, ll], 1), jnp.concatenate([rh, rh], 0)) + dot(lh, rl)


def silu(value):
    return value / (1.0 + jnp.exp(-value))


ANY = pl.BlockSpec(memory_space=pl.ANY)
KEPT = (
    ((C, C), F32),
    ((BLOCKS * HEADS, C), F32),
    ((BLOCKS * HEADS, C, C), F32),
    ((BLOCKS * KEYS, C, 2 * DK), BF16),
    ((BLOCKS * HEADS, C, 2 * DV + 2 * DK), BF16),
    ((HEADS, DK, DK), BF16),
    ((HEADS, DK, 2 * DV), BF16),
)


def shape(dims, kind):
    return jax.ShapeDtypeStruct(dims, kind)


def my_core():
    return lax.rem(lax.axis_index("seq"), 2)


def params(mib):
    return pltpu.CompilerParams(vmem_limit_bytes=mib * 2**20)


def cost(flops, moved):
    return pl.CostEstimate(flops=flops, bytes_accessed=moved, transcendentals=0)


def cut_kernel(raw, gate, decay, beta, weight, give, tail, half, rows, decays, betas, sems):
    core = my_core()
    copies = []

    def copy(source, target):
        copies.append(pltpu.make_async_copy(source, target, sems.at[len(copies)]))
        copies[-1].start()

    def cut(ref, first, width, part, at=0, count=C):
        column = pl.multiple_of(first + part * width, width)
        return ref.at[at : at + count, pl.ds(column, width)]

    copy(decay, decays)
    copy(beta, betas)
    parts = ((0, QK, 0), (2 * QK, QK, QK), (4 * QK, HEADS * DV, 2 * QK))
    for first, width, to in parts:
        copy(cut(raw, first, width, 1 - core), give.at[0:C, to : to + width])
    copy(cut(gate, 0, HEADS * DV, 1 - core), give.at[0:C, RAW:ROW])
    for first, width, to in parts:
        copy(cut(raw, first, width, core, C - 16, 16), tail.at[:, to : to + width])
    copy(cut(weight, 0, HALF, core), half)
    give[C:TALL, 2 * C :] = jnp.zeros((16, ROW - 2 * C), BF16)
    copies[0].wait()
    copies[1].wait()
    for at, codes in ((0, decays), (C, betas)):
        code = codes[pl.ds(pl.multiple_of((1 - core) * HEADS, HEADS), HEADS), :]
        rows[0:HEADS, at : at + C] = (code >> 4).astype(F32)
        rows[HEADS:16, at : at + C] = (code & 15).astype(F32)
    give[C:TALL, 0 : 2 * C] = rows[...].astype(BF16)
    for one in copies[2:]:
        one.wait()


def cut_rows(raw, gate, decay, beta, weight):
    return pl.pallas_call(
        cut_kernel,
        out_shape=[
            shape((TALL, ROW), BF16),
            shape((16, RAW), BF16),
            shape((weight.shape[0], HALF), BF16),
        ],
        in_specs=[ANY] * 5,
        out_specs=[VMEM] * 3,
        scratch_shapes=[
            pltpu.VMEM((16, 2 * C), F32),
            pltpu.VMEM((VH, C), jnp.int32),
            pltpu.VMEM((VH, C), jnp.int32),
            pltpu.SemaphoreType.DMA((10,)),
        ],
        compiler_params=params(60),
        name="cut",
    )(raw, gate, decay, beta, weight)


def assemble(core, staged, halo, raw, first, width):
    at = slice(first, first + width)
    raw[0:8] = halo[:, at].astype(F32)[8:16]
    for i, block in enumerate((core, 1 - core)):
        raw[pl.ds(pl.multiple_of(8 + block * C, 8), C)] = staged[i].astype(F32)


def convolved(raw, taps, at, channel, j):
    weights = taps[:, pl.ds(pl.multiple_of(channel, DK), DK)]
    base = 8 + j * C - 3
    total = weights[0:1] * raw[base : base + C, at : at + DK]
    for t in range(1, 4):
        total = total + weights[t : t + 1] * raw[base + t : base + t + C, at : at + DK]
    return silu(total)


def over_length(value):
    return lax.rsqrt(jnp.sum(value * value, -1, keepdims=True) + 1e-06)


def unit_of(j, h):
    return j * HEADS + h


def column(columns, kind, unit):
    at = kind * BLOCKS * HEADS + unit
    return columns[:, at : at + 1]


def terms_kernel(
    scale_log, bias, decay_codes, beta_codes, own, got, halo, taps,
    message, *rest,
):
    outs, kept, rest = rest[: len(KEPT)], rest[len(KEPT) : 2 * len(KEPT)], rest[2 * len(KEPT) :]
    raw, staged, their_codes, decay, beta, joins, keys_t, rights, transit, arrive, sems = rest
    columns, starts, pairs, keys_out, solved_out, early_transit, early_add = kept
    core = my_core()
    copies = []
    column_of = pl.multiple_of(2 * QK + core * QK, QK), pl.multiple_of(4 * QK + core * HEADS * DV, HEADS * DV)
    loads = [
        pltpu.make_async_copy(*one, arrive.at[i])
        for i, one in enumerate((
            (own.at[:, pl.ds(column_of[0], QK)], staged.at[0, :, 0:QK]),
            (own.at[:, pl.ds(column_of[1], HEADS * DV)], staged.at[0, :, QK:]),
            (got.at[0:C, QK:RAW], staged.at[1]),
            (got.at[C:TALL, 0 : 2 * C], their_codes),
        ))
    ]
    for one in loads:
        one.start()

    def leave(which, first=0, count=None):
        source, target = kept[which], outs[which]
        if count:
            source, target = source.at[first : first + count], target.at[first : first + count]
        copies.append(pltpu.make_async_copy(source, target, sems.at[len(copies)]))
        copies[-1].start()

    loads[3].wait()
    codes = their_codes[...].astype(F32)
    ours = pl.ds(pl.multiple_of(core * HEADS, HEADS), HEADS)
    theirs = pl.ds(pl.multiple_of((1 - core) * HEADS, HEADS), HEADS)
    decay[ours, :] = decay_codes[ours, :].astype(F32)
    beta[ours, :] = beta_codes[ours, :].astype(F32)
    decay[theirs, :] = 16.0 * codes[0:HEADS, 0:C] + codes[HEADS:16, 0:C]
    beta[theirs, :] = 16.0 * codes[0:HEADS, C:] + codes[HEADS:16, C:]

    def by_head(ref):
        rows = [jnp.full((1, C), ref[core * HEADS + h], F32) for h in range(HEADS)]
        return jnp.concatenate(rows * BLOCKS, 0)

    level = decay[...] / 32.0 - 16.0 + by_head(bias)
    small = jnp.exp(-jnp.abs(level))
    one_more = 1.0 + small
    gap = one_more - 1.0
    log1p = jnp.where(gap == 0.0, small, jnp.log(one_more) * (small / jnp.where(gap == 0.0, 1.0, gap)))
    log_decay = -jnp.exp(by_head(scale_log)) * (jnp.maximum(level, 0.0) + log1p)
    row_ids = lax.broadcasted_iota(jnp.int32, (C, C), 0)
    col_ids = lax.broadcasted_iota(jnp.int32, (C, C), 1)
    sums = jnp.dot(
        log_decay,
        (row_ids <= col_ids).astype(F32),
        precision=lax.Precision.HIGHEST,
        preferred_element_type=F32,
    )
    strength = 1.0 / (1.0 + jnp.exp(8.0 - beta[...] / 32.0))
    start = jnp.exp(sums)
    starts[...] = start
    end = jnp.exp(sums[:, C - 1 : C] - sums)
    columns[...] = jnp.concatenate(
        [sums, strength, start, end, strength * start, jnp.zeros((C - 5 * BLOCKS * HEADS, C), F32)], 0
    ).T

    leave(0)
    leave(1)
    inclusive = row_ids >= col_ids
    strict = row_ids > col_ids
    eye = (row_ids == col_ids).astype(BF16)
    for k in range(1, 7):
        joins[k - 1] = (
            ((row_ids >> (k + 1)) == (col_ids >> (k + 1))) & ((row_ids >> k) != (col_ids >> k))
        ).astype(F32).astype(BF16)
    near = (row_ids >> 1) == (col_ids >> 1)

    for one in loads[:3]:
        one.wait()
    assemble(core, staged, halo, raw, QK, RAW - QK)
    units = range(BLOCKS * HEADS)
    lowers, inverses = [], []
    for j in range(BLOCKS):
        for g in range(KEYS):
            keys = convolved(raw, taps, g * DK, 2 * QK + core * QK + g * DK, j)
            keys = keys * over_length(keys)
            kh, kl = split(keys)
            keys_out[j * KEYS + g, :, :DK] = kh
            keys_out[j * KEYS + g, :, DK:] = kl
            kh_t, kl_t = split(keys.T)
            keys_t[j * KEYS + g, :, :C] = kh_t
            keys_t[j * KEYS + g, :, C:] = kl_t
            gram = dot_t(kh, kh)
            for h in (2 * g, 2 * g + 1):
                u = unit_of(j, h)
                pair = jnp.where(inclusive, jnp.exp(jnp.minimum(column(columns, 0, u) - sums[u : u + 1], 0.0)), 0.0)
                pairs[u] = pair
                lower = jnp.where(strict, column(columns, 1, u) * pair * gram, 0.0)
                lowers.append(lower.astype(BF16))
                inverses.append(eye - jnp.where(near, lower, 0.0).astype(BF16))
                values = convolved(raw, taps, QK + h * DV, 4 * QK + core * HEADS * DV + h * DV, j)
                rights[u, :, :DV] = column(columns, 1, u) * values
                rights[u, :, DV:] = column(columns, 4, u) * keys
        leave(2, j * HEADS, HEADS)
        leave(3, j * KEYS, KEYS)
    for k in range(6):
        halves = [dot(lowers[u] * joins[k], inverses[u]).astype(BF16) for u in units]
        inverses = [inverses[u] - dot(inverses[u], halves[u]).astype(BF16) for u in units]
    for u in units:
        j, h = u // HEADS, u % HEADS
        solved = rights[u] + dot(inverses[u] - eye, rights[u].astype(BF16))
        values, writes = solved[:, :DV], solved[:, DV:]
        high, low = split(values)
        solved_out[u, :, :DV] = high
        solved_out[u, :, DV : 2 * DV] = low
        high, low = split(writes)
        solved_out[u, :, 2 * DV : 2 * DV + DK] = high
        solved_out[u, :, 2 * DV + DK :] = low
        leave(4, u, 1)
        g = j * KEYS + h // 2
        kt = keys_t[g, :, :C], keys_t[g, :, C:]
        moved = dot3(kt, split(column(columns, 3, u) * writes))
        add = dot3(kt, split(column(columns, 3, u) * values))
        last = start[u : u + 1, C - 1 : C]
        if j == 0:
            transit[h] = moved
            early_transit[h] = moved.astype(BF16)
            add_high, add_low = split(add)
            early_add[h, :, :DV] = add_high
            early_add[h, :, DV:] = add_low
        else:
            first = start[unit_of(0, h) : unit_of(0, h) + 1, C - 1 : C]
            second = moved.astype(BF16)
            crossed = dot(second, jnp.concatenate([early_transit[h], early_add[h, :, :DV]], 1))
            earlier = early_add[h, :, :DV].astype(F32) + early_add[h, :, DV:].astype(F32)
            message[h, 0:DK] = (last * transit[h] + first * moved - crossed[:, :DK]).astype(BF16)
            message[h, DK : 2 * DK] = (last * earlier - crossed[:, DK:] + add).astype(BF16)
            both = jnp.broadcast_to(first * last, (1, DK))
            top = both.astype(BF16).astype(F32)
            middle = (both - top).astype(BF16).astype(F32)
            parts = jnp.concatenate([top, middle, both - top - middle, jnp.zeros((13, DK), F32)], 0)
            message[h, 2 * DK : WHOLE] = parts.astype(BF16)
        if u == HEADS - 1:
            leave(5)
            leave(6)
    for one in copies:
        one.wait()


def run_terms(*operands):
    units = BLOCKS * HEADS
    return pl.pallas_call(
        terms_kernel,
        out_shape=[shape((HEADS, WHOLE, DV), BF16)] + [shape(*one) for one in KEPT],
        in_specs=[SMEM] * 2 + [VMEM] * 2 + [ANY] * 2 + [VMEM] * 2,
        out_specs=[VMEM] + [ANY] * len(KEPT),
        scratch_shapes=[pltpu.VMEM(*one) for one in KEPT]
        + [
            pltpu.VMEM((8 + BLOCKS * C, RAW - QK), F32),
            pltpu.VMEM((BLOCKS, C, RAW - QK), BF16),
            pltpu.VMEM((16, 2 * C), BF16),
            pltpu.VMEM((units, C), F32),
            pltpu.VMEM((units, C), F32),
            pltpu.VMEM((6, C, C), BF16),
            pltpu.VMEM((BLOCKS * KEYS, DK, 2 * C), BF16),
            pltpu.VMEM((units, C, DV + DK), F32),
            pltpu.VMEM((HEADS, DK, DK), F32),
            pltpu.SemaphoreType.DMA((4,)),
            pltpu.SemaphoreType.DMA((24,)),
        ],
        compiler_params=params(TERMS_MIB),
        cost_estimate=cost(8 * 10**9, 2**25),
        name="terms",
    )(*operands)


def reads_kernel(own, got, halo, taps, *rest):
    sources, (base, reads), kept = rest[: len(KEPT)], rest[len(KEPT) : len(KEPT) + 2], rest[len(KEPT) + 2 : -5]
    bases, readers, raw, staged, sems = rest[-5:]
    core = my_core()
    columns, starts, pairs, keys, solved, early_transit, early_add = kept
    copies = []

    def move(source, target, first=None, count=HEADS):
        if first is not None:
            source, target = source.at[first : first + count], target.at[first : first + count]
        copies.append(pltpu.make_async_copy(source, target, sems.at[len(copies)]))
        copies[-1].start()

    move(own.at[:, pl.ds(pl.multiple_of(core * QK, QK), QK)], staged.at[0])
    move(got.at[0:C, 0:QK], staged.at[1])
    for i in (0, 1, 3):
        move(sources[i], kept[i])
    for j in range(BLOCKS):
        move(sources[2], pairs, j * HEADS)
        move(sources[4], solved, j * HEADS)
        if j == 0:
            move(sources[5], early_transit)
            move(sources[6], early_add)
    for one in copies[:5]:
        one.wait()
    assemble(core, staged, halo, raw, 0, QK)
    for j in range(BLOCKS):
        for one in copies[5:7] if j == 0 else copies[7:11]:
            one.wait()
        for g in range(KEYS):
            queries = convolved(raw, taps, g * DK, core * QK + g * DK, j)
            queries = queries * (over_length(queries) * (1.0 / math.sqrt(DK)))
            qh, ql = split(queries)
            both = keys[j * KEYS + g]
            kh, kl = both[:, :DK], both[:, DK:]
            plain = dot_t(jnp.concatenate([qh, ql], 1), jnp.concatenate([kh, kh], 1)) + dot_t(qh, kl)
            for h in (2 * g, 2 * g + 1):
                u = unit_of(j, h)
                gram = split(pairs[u] * plain)
                inner = solved[u]
                out = dot3(gram, (inner[:, :DV], inner[:, DV : 2 * DV]))
                writes = inner[:, 2 * DV : 2 * DV + DK], inner[:, 2 * DV + DK :]
                read = column(columns, 2, u) * queries - dot3(gram, writes)
                if j:
                    high, low = split(read)
                    out = out + dot3((high, low), (early_add[h, :, :DV], early_add[h, :, DV:]))
                    before = unit_of(0, h)
                    read = starts[before : before + 1, C - 1 : C] * read - dot(high, early_transit[h])
                bases[u] = out
                high, low = split(read)
                readers[u, :, :DK] = high
                readers[u, :, DK:] = low
        move(bases, base, j * HEADS)
        move(readers, reads, j * HEADS)
    for one in copies[11:]:
        one.wait()


def run_reads(*operands):
    units = BLOCKS * HEADS
    return pl.pallas_call(
        reads_kernel,
        out_shape=[shape((units, C, DV), F32), shape((units, C, 2 * DK), BF16)],
        in_specs=[ANY] * 2 + [VMEM] * 2 + [ANY] * len(KEPT),
        out_specs=[ANY] * 2,
        scratch_shapes=[pltpu.VMEM(*one) for one in KEPT]
        + [
            pltpu.VMEM((units, C, DV), F32),
            pltpu.VMEM((units, C, 2 * DK), BF16),
            pltpu.VMEM((8 + BLOCKS * C, QK), F32),
            pltpu.VMEM((BLOCKS, C, QK), BF16),
            pltpu.SemaphoreType.DMA((15,)),
        ],
        compiler_params=params(TERMS_MIB),
        cost_estimate=cost(4 * 10**9, 2**24),
        name="reads",
    )(*operands)


def enter_kernel(arrived, entering, messages, sems):
    copies = [
        pltpu.make_async_copy(arrived.at[chip], messages.at[chip], sems.at[chip]) for chip in range(CHIPS - 1)
    ]
    for one in copies:
        one.start()
    state = jnp.zeros((DK, DV), F32)
    for chip in range(CHIPS):
        high = state.astype(BF16)
        entering[chip] = high
        if chip < CHIPS - 1:
            copies[chip].wait()
            parts = messages[chip, 2 * DK : WHOLE].astype(F32)
            factor = parts[0:1] + parts[1:2] + parts[2:3]
            state = factor * state - dot(messages[chip, 0:DK], high) + messages[chip, DK : 2 * DK].astype(F32)


def run_enter(messages):
    return pl.pallas_call(
        enter_kernel,
        out_shape=shape((CHIPS, DK, DV), BF16),
        in_specs=[ANY],
        out_specs=VMEM,
        scratch_shapes=[pltpu.VMEM((CHIPS, WHOLE, DV), BF16), pltpu.SemaphoreType.DMA((CHIPS - 1,))],
        compiler_params=params(TERMS_MIB),
        cost_estimate=cost(10**9, 2**20),
        name="enter",
    )(messages)


def finish_kernel(arrived, base, reads, gate, got, gain, mine, theirs, entering, bases, readers, gates, sems):
    core = my_core()
    blocks = 1 - core, core
    loads = [pltpu.make_async_copy(arrived, entering, sems.at[6])]
    loads[0].start()
    for i, block in enumerate(blocks):
        units = pl.ds(pl.multiple_of(block * HEADS, HEADS), HEADS)
        column_of = pl.multiple_of(core * HEADS * DV, HEADS * DV)
        a_gate = gate.at[:, pl.ds(column_of, HEADS * DV)] if i else got.at[0:C, RAW:ROW]
        for source, target in ((a_gate, gates), (reads.at[units], readers), (base.at[units], bases)):
            loads.append(pltpu.make_async_copy(source, target.at[i], sems.at[len(loads) - 1]))
            loads[-1].start()
    for i, out in enumerate((theirs, mine)):
        for one in loads[4:] if i else loads[:4]:
            one.wait()
        for h in range(HEADS):
            state = entering[h]
            rows = bases[i, h] + dot(readers[i, h], jnp.concatenate([state, state], 0))
            square_mean = jnp.mean(rows * rows, -1, keepdims=True)
            opening = silu(gates[i, :, h * DV : (h + 1) * DV].astype(F32))
            out[h] = (rows * lax.rsqrt(square_mean + 1e-06) * gain[...] * opening).astype(BF16)


def run_finish(entering, base, reads, gate, got, gain):
    return pl.pallas_call(
        finish_kernel,
        out_shape=[shape((HEADS, C, DV), BF16)] * 2,
        in_specs=[ANY] * 5 + [VMEM],
        out_specs=[VMEM] * 2,
        scratch_shapes=[
            pltpu.VMEM((HEADS, DK, DV), BF16),
            pltpu.VMEM((BLOCKS, HEADS, C, DV), F32),
            pltpu.VMEM((BLOCKS, HEADS, C, 2 * DK), BF16),
            pltpu.VMEM((BLOCKS, C, HEADS * DV), BF16),
            pltpu.SemaphoreType.DMA((7,)),
        ],
        compiler_params=params(TERMS_MIB),
        cost_estimate=cost(2 * 10**9, 2**22),
        name="finish",
    )(entering, base, reads, gate, got, gain)


def in_order_of(core, heads, ordered):
    row = lax.axis_index("fsdp")
    y, x = row // SIDE, lax.rem(row, SIDE)
    for second in range(SIDE):
        for first in range(SIDE):
            back_x = jnp.where(core == 0, first, second)
            back_y = jnp.where(core == 0, second, first)
            head = lax.rem(y - back_y + SIDE, SIDE) * SIDE + lax.rem(x - back_x + SIDE, SIDE)
            at = (second * SIDE + first) * DV
            ordered[:, at : at + DV] = heads[head]


def product_of(ordered, weights):
    width = SIDE * DV
    total = dot(ordered[:, :width], weights[0][...].reshape(width, HALF))
    for second in range(1, SIDE):
        at = second * width
        total = total + dot(ordered[:, at : at + width], weights[second][...].reshape(width, HALF))
    return total.astype(BF16)


def project_kernel(mine, theirs, *rest):
    own, others, (out, normed, ordered, sems) = rest[:SIDE], rest[SIDE : 2 * SIDE], rest[2 * SIDE :]
    core = my_core()
    loads = []
    for i, (source, its_core) in enumerate(((mine, core), (theirs, 1 - core))):
        target = normed.at[pl.ds(pl.multiple_of(its_core * HEADS, HEADS), HEADS)]
        loads.append(pltpu.make_async_copy(source, target, sems.at[i]))
        loads[-1].start()
    for one in loads:
        one.wait()
    for its_core, weights in ((core, own), (1 - core, others)):
        in_order_of(its_core, normed, ordered)
        out[:, pl.ds(pl.multiple_of(its_core * HALF, HALF), HALF)] = product_of(ordered, weights)


def project(mine, theirs, weights, other_weights):
    return pl.pallas_call(
        project_kernel,
        out_shape=shape((C, WIDTH), BF16),
        in_specs=[ANY] * 2 + [VMEM] * 2 * SIDE,
        out_specs=VMEM,
        compiler_params=params(40),
        cost_estimate=cost(2 * C * WIDTH * WIDTH, 2**23),
        scratch_shapes=[
            pltpu.VMEM((VH, C, DV), BF16),
            pltpu.VMEM((C, WIDTH), BF16),
            pltpu.SemaphoreType.DMA((2,)),
        ],
        name="project",
    )(mine, theirs, *weights, *other_weights)


def along(block, distance, second):
    route = []
    for i in range(SEGMENTS):
        by_x = (i % 2 == 0) != second
        for y in range(SIDE):
            for x in range(SIDE):
                to_y, to_x = (y, (x + distance) % SIDE) if by_x else ((y + distance) % SIDE, x)
                route.append(((i * SIDE + y) * SIDE + x, (i * SIDE + to_y) * SIDE + to_x))
    return lax.ppermute(block, ("seq", "fsdp"), route)


def local(
    qkv_raw,
    output_gate,
    decay_codes,
    beta_codes,
    conv_weight,
    decay_scale_log,
    decay_bias,
    norm_gain,
    out_weight,
):
    barrier = lax.optimization_barrier
    raw, decay, beta = qkv_raw[0], decay_codes[0], beta_codes[0]
    give, tail, half = cut_rows(raw, output_gate[0], decay, beta, out_weight)
    got = other_core(give)
    tail = jnp.where(lax.axis_index("seq") % 2 == 0, got[C - 16 : C, :RAW], tail)
    halo = lax.ppermute(tail, "seq", [(i, i + 2) for i in range(SEGMENTS - 2)])
    parts = [along(half, distance, False) for distance in (1, 2, 3)]
    message, *kept = run_terms(
        decay_scale_log, decay_bias, decay, beta, raw, got, halo, conv_weight
    )
    message, half, *parts = barrier((message, half, *parts))
    messages = between_chips(message)
    line = jnp.stack([half, *parts])
    later = [along(line, distance, True) for distance in (1, 2, 3)]
    other_line = other_core(line)
    base, reads = run_reads(raw, got, halo, conv_weight, *kept)
    messages, base, reads = barrier((messages, base, reads))
    entering = between_chips(run_enter(messages))
    entering, *later = barrier((entering, *later))
    other_weights = [other_line] + [other_core(weight) for weight in later]
    mine, theirs = run_finish(entering, base, reads, output_gate[0], got, norm_gain[None])
    return project(mine, other_core(theirs), [line, *later], other_weights)[None]


def solution(mesh):
    return jax.shard_map(
        local,
        mesh=mesh,
        in_specs=(
            P("fsdp", "seq", None),
            P("fsdp", "seq", None),
            P("fsdp", None, "seq"),
            P("fsdp", None, "seq"),
            P(),
            P(),
            P(),
            P(),
            P("fsdp", None),
        ),
        out_specs=P("fsdp", "seq", None),
        check_vma=False,
    )
```

```python
import math

import jax
import jax.numpy as jnp
from jax import lax
from jax.experimental import pallas as pl
from jax.experimental.pallas import tpu as pltpu
from jax.sharding import PartitionSpec as P


CHIPS = 8
SEGMENTS = 16
C = 128
DK = 128
DV = 128
VH = 16
HEADS = 8
KEYS = 4
BLOCKS = 2
WIDTH = 2048
HALF = 1024
QK = KEYS * DK
RAW = 2 * QK + HEADS * DV
ROW = RAW + HEADS * DV
TALL = C + 16
TERMS_MIB = 60
WHOLE = 2 * DK + 16
SIDE = 4
F32 = jnp.float32
BF16 = jnp.bfloat16
VMEM = pl.BlockSpec(memory_space=pltpu.VMEM)
SMEM = pl.BlockSpec(memory_space=pltpu.SMEM)


def to_chip(block, distance):
    return lax.ppermute(
        block, "seq", [(i, (i + 2 * distance) % SEGMENTS) for i in range(SEGMENTS)]
    )


def other_core(block):
    return lax.ppermute(block, "seq", [(i, i ^ 1) for i in range(SEGMENTS)])


def between_chips(blocks):
    groups = [[2 * z + c for z in range(CHIPS)] for c in range(2)]
    return lax.all_to_all(blocks, "seq", 0, 0, axis_index_groups=groups)


def dot(left, right):
    return jnp.dot(left, right, preferred_element_type=F32)


def dot_t(left, right):
    return lax.dot_general(
        left, right, (((1,), (1,)), ((), ())), preferred_element_type=F32
    )


def split(value):
    high = value.astype(BF16)
    return high, (value - high.astype(F32)).astype(BF16)


def dot3(left, right):
    lh, ll = left
    rh, rl = right
    return dot(jnp.concatenate([lh, ll], 1), jnp.concatenate([rh, rh], 0)) + dot(lh, rl)


def silu(value):
    return value / (1.0 + jnp.exp(-value))


ANY = pl.BlockSpec(memory_space=pl.ANY)
KEPT = (
    ((C, C), F32),
    ((BLOCKS * HEADS, C), F32),
    ((BLOCKS * KEYS, C, 2 * DK), BF16),
    ((BLOCKS * HEADS, C, 2 * DV + 2 * DK), BF16),
    ((HEADS, DK, DK), BF16),
    ((HEADS, DK, 2 * DV), BF16),
)


def shape(dims, kind):
    return jax.ShapeDtypeStruct(dims, kind)


def my_core():
    return lax.rem(lax.axis_index("seq"), 2)


def params(mib):
    return pltpu.CompilerParams(vmem_limit_bytes=mib * 2**20)


def cost(flops, moved):
    return pl.CostEstimate(flops=flops, bytes_accessed=moved, transcendentals=0)


def cut_kernel(raw, gate, decay, beta, weight, give, tail, half, rows, decays, betas, sems):
    core = my_core()
    copies = []

    def copy(source, target):
        copies.append(pltpu.make_async_copy(source, target, sems.at[len(copies)]))
        copies[-1].start()

    def cut(ref, first, width, part, at=0, count=C):
        column = pl.multiple_of(first + part * width, width)
        return ref.at[at : at + count, pl.ds(column, width)]

    copy(decay, decays)
    copy(beta, betas)
    parts = ((0, QK, 0), (2 * QK, QK, QK), (4 * QK, HEADS * DV, 2 * QK))
    for first, width, to in parts:
        copy(cut(raw, first, width, 1 - core), give.at[0:C, to : to + width])
    copy(cut(gate, 0, HEADS * DV, 1 - core), give.at[0:C, RAW:ROW])
    for first, width, to in parts:
        copy(cut(raw, first, width, core, C - 16, 16), tail.at[:, to : to + width])
    copy(cut(weight, 0, HALF, core), half)
    give[C:TALL, 2 * C :] = jnp.zeros((16, ROW - 2 * C), BF16)
    copies[0].wait()
    copies[1].wait()
    for at, codes in ((0, decays), (C, betas)):
        code = codes[pl.ds(pl.multiple_of((1 - core) * HEADS, HEADS), HEADS), :]
        rows[0:HEADS, at : at + C] = (code >> 4).astype(F32)
        rows[HEADS:16, at : at + C] = (code & 15).astype(F32)
    give[C:TALL, 0 : 2 * C] = rows[...].astype(BF16)
    for one in copies[2:]:
        one.wait()


def cut_rows(raw, gate, decay, beta, weight):
    return pl.pallas_call(
        cut_kernel,
        out_shape=[
            shape((TALL, ROW), BF16),
            shape((16, RAW), BF16),
            shape((weight.shape[0], HALF), BF16),
        ],
        in_specs=[ANY] * 5,
        out_specs=[VMEM] * 3,
        scratch_shapes=[
            pltpu.VMEM((16, 2 * C), F32),
            pltpu.VMEM((VH, C), jnp.int32),
            pltpu.VMEM((VH, C), jnp.int32),
            pltpu.SemaphoreType.DMA((10,)),
        ],
        compiler_params=params(60),
        name="cut",
    )(raw, gate, decay, beta, weight)


def assemble(core, staged, halo, raw, first, at, width):
    to = slice(at, at + width)
    raw[0:8, to] = halo[:, first + at : first + at + width].astype(F32)[8:16]
    for i, block in enumerate((core, 1 - core)):
        raw[pl.ds(pl.multiple_of(8 + block * C, 8), C), to] = staged[i, :, to].astype(F32)


def convolved(raw, taps, at, channel, j):
    weights = taps[:, pl.ds(pl.multiple_of(channel, DK), DK)]
    base = 8 + j * C - 3
    total = weights[0:1] * raw[base : base + C, at : at + DK]
    for t in range(1, 4):
        total = total + weights[t : t + 1] * raw[base + t : base + t + C, at : at + DK]
    return silu(total)


def over_length(value):
    return lax.rsqrt(jnp.sum(value * value, -1, keepdims=True) + 1e-06)


def unit_of(j, h):
    return j * HEADS + h


def column(columns, kind, unit):
    at = kind * BLOCKS * HEADS + unit
    return columns[:, at : at + 1]


def terms_kernel(
    scale_log, bias, decay_codes, beta_codes, own, got, halo, taps,
    message, *rest,
):
    outs, kept, rest = rest[: len(KEPT)], rest[len(KEPT) : 2 * len(KEPT)], rest[2 * len(KEPT) :]
    raw, staged, their_codes, decay, beta, joins, keys_t, rights, transit, arrive, sems = rest
    columns, totals, keys_out, solved_out, early_transit, early_add = kept
    core = my_core()
    copies = []
    column_of = pl.multiple_of(2 * QK + core * QK, QK), pl.multiple_of(4 * QK + core * HEADS * DV, HEADS * DV)
    loads = [
        pltpu.make_async_copy(*one, arrive.at[i])
        for i, one in enumerate((
            (got.at[C:TALL, 0 : 2 * C], their_codes),
            (own.at[:, pl.ds(column_of[0], QK)], staged.at[0, :, 0:QK]),
            (got.at[0:C, QK : 2 * QK], staged.at[1, :, 0:QK]),
            (own.at[:, pl.ds(column_of[1], HEADS * DV)], staged.at[0, :, QK:]),
            (got.at[0:C, 2 * QK : RAW], staged.at[1, :, QK:]),
        ))
    ]
    for one in loads:
        one.start()

    def leave(which, first=0, count=None):
        source, target = kept[which], outs[which]
        if count:
            source, target = source.at[first : first + count], target.at[first : first + count]
        copies.append(pltpu.make_async_copy(source, target, sems.at[len(copies)]))
        copies[-1].start()

    loads[0].wait()
    codes = their_codes[...].astype(F32)
    ours = pl.ds(pl.multiple_of(core * HEADS, HEADS), HEADS)
    theirs = pl.ds(pl.multiple_of((1 - core) * HEADS, HEADS), HEADS)
    decay[ours, :] = decay_codes[ours, :].astype(F32)
    beta[ours, :] = beta_codes[ours, :].astype(F32)
    decay[theirs, :] = 16.0 * codes[0:HEADS, 0:C] + codes[HEADS:16, 0:C]
    beta[theirs, :] = 16.0 * codes[0:HEADS, C:] + codes[HEADS:16, C:]

    def by_head(ref):
        rows = [jnp.full((1, C), ref[core * HEADS + h], F32) for h in range(HEADS)]
        return jnp.concatenate(rows * BLOCKS, 0)

    level = decay[...] / 32.0 - 16.0 + by_head(bias)
    small = jnp.exp(-jnp.abs(level))
    one_more = 1.0 + small
    gap = one_more - 1.0
    log1p = jnp.where(gap == 0.0, small, jnp.log(one_more) * (small / jnp.where(gap == 0.0, 1.0, gap)))
    log_decay = -jnp.exp(by_head(scale_log)) * (jnp.maximum(level, 0.0) + log1p)
    row_ids = lax.broadcasted_iota(jnp.int32, (C, C), 0)
    col_ids = lax.broadcasted_iota(jnp.int32, (C, C), 1)
    sums = jnp.dot(
        log_decay,
        (row_ids <= col_ids).astype(F32),
        precision=lax.Precision.HIGHEST,
        preferred_element_type=F32,
    )
    strength = 1.0 / (1.0 + jnp.exp(8.0 - beta[...] / 32.0))
    start = jnp.exp(sums)
    totals[...] = sums
    end = jnp.exp(sums[:, C - 1 : C] - sums)
    columns[...] = jnp.concatenate(
        [sums, strength, start, end, strength * start, jnp.zeros((C - 5 * BLOCKS * HEADS, C), F32)], 0
    ).T

    leave(0)
    leave(1)
    inclusive = row_ids >= col_ids
    strict = row_ids > col_ids
    eye = (row_ids == col_ids).astype(BF16)
    for k in range(1, 7):
        joins[k - 1] = (
            ((row_ids >> (k + 1)) == (col_ids >> (k + 1))) & ((row_ids >> k) != (col_ids >> k))
        ).astype(F32).astype(BF16)
    near = (row_ids >> 1) == (col_ids >> 1)

    for one in loads[1:3]:
        one.wait()
    assemble(core, staged, halo, raw, QK, 0, QK)
    units = range(BLOCKS * HEADS)
    lowers, inverses = [], []
    for j in range(BLOCKS):
        for g in range(KEYS):
            keys = convolved(raw, taps, g * DK, 2 * QK + core * QK + g * DK, j)
            keys = keys * over_length(keys)
            kh, kl = split(keys)
            keys_out[j * KEYS + g, :, :DK] = kh
            keys_out[j * KEYS + g, :, DK:] = kl
            kh_t, kl_t = split(keys.T)
            keys_t[j * KEYS + g, :, :C] = kh_t
            keys_t[j * KEYS + g, :, C:] = kl_t
            gram = dot_t(kh, kh)
            for h in (2 * g, 2 * g + 1):
                u = unit_of(j, h)
                pair = jnp.where(inclusive, jnp.exp(jnp.minimum(column(columns, 0, u) - sums[u : u + 1], 0.0)), 0.0)
                lower = jnp.where(strict, column(columns, 1, u) * pair * gram, 0.0)
                lowers.append(lower.astype(BF16))
                inverses.append(eye - jnp.where(near, lower, 0.0).astype(BF16))
                rights[u, :, DV:] = column(columns, 4, u) * keys
        leave(2, j * KEYS, KEYS)
    for one in loads[3:]:
        one.wait()
    assemble(core, staged, halo, raw, QK, QK, HEADS * DV)
    for k in range(6):
        for u in units[3 * k : 3 * k + 3]:
            j, h = u // HEADS, u % HEADS
            values = convolved(raw, taps, QK + h * DV, 4 * QK + core * HEADS * DV + h * DV, j)
            rights[u, :, :DV] = column(columns, 1, u) * values
        halves = [dot(lowers[u] * joins[k], inverses[u]).astype(BF16) for u in units]
        inverses = [inverses[u] - dot(inverses[u], halves[u]).astype(BF16) for u in units]
    for u in units:
        j, h = u // HEADS, u % HEADS
        solved = rights[u] + dot(inverses[u] - eye, rights[u].astype(BF16))
        values, writes = solved[:, :DV], solved[:, DV:]
        high, low = split(values)
        solved_out[u, :, :DV] = high
        solved_out[u, :, DV : 2 * DV] = low
        high, low = split(writes)
        solved_out[u, :, 2 * DV : 2 * DV + DK] = high
        solved_out[u, :, 2 * DV + DK :] = low
        leave(3, u, 1)
        g = j * KEYS + h // 2
        kt = keys_t[g, :, :C], keys_t[g, :, C:]
        moved = dot3(kt, split(column(columns, 3, u) * writes))
        add = dot3(kt, split(column(columns, 3, u) * values))
        last = start[u : u + 1, C - 1 : C]
        if j == 0:
            transit[h] = moved
            early_transit[h] = moved.astype(BF16)
            add_high, add_low = split(add)
            early_add[h, :, :DV] = add_high
            early_add[h, :, DV:] = add_low
        else:
            first = start[unit_of(0, h) : unit_of(0, h) + 1, C - 1 : C]
            second = moved.astype(BF16)
            crossed = dot(second, jnp.concatenate([early_transit[h], early_add[h, :, :DV]], 1))
            earlier = early_add[h, :, :DV].astype(F32) + early_add[h, :, DV:].astype(F32)
            message[h, 0:DK] = (last * transit[h] + first * moved - crossed[:, :DK]).astype(BF16)
            message[h, DK : 2 * DK] = (last * earlier - crossed[:, DK:] + add).astype(BF16)
            both = jnp.broadcast_to(first * last, (1, DK))
            top = both.astype(BF16).astype(F32)
            middle = (both - top).astype(BF16).astype(F32)
            parts = jnp.concatenate([top, middle, both - top - middle, jnp.zeros((13, DK), F32)], 0)
            message[h, 2 * DK : WHOLE] = parts.astype(BF16)
        if u == HEADS - 1:
            leave(4)
            leave(5)
    for one in copies:
        one.wait()


def run_terms(*operands):
    units = BLOCKS * HEADS
    return pl.pallas_call(
        terms_kernel,
        out_shape=[shape((HEADS, WHOLE, DV), BF16)] + [shape(*one) for one in KEPT],
        in_specs=[SMEM] * 2 + [VMEM] * 2 + [ANY] * 2 + [VMEM] * 2,
        out_specs=[VMEM] + [ANY] * len(KEPT),
        scratch_shapes=[pltpu.VMEM(*one) for one in KEPT]
        + [
            pltpu.VMEM((8 + BLOCKS * C, RAW - QK), F32),
            pltpu.VMEM((BLOCKS, C, RAW - QK), BF16),
            pltpu.VMEM((16, 2 * C), BF16),
            pltpu.VMEM((units, C), F32),
            pltpu.VMEM((units, C), F32),
            pltpu.VMEM((6, C, C), BF16),
            pltpu.VMEM((BLOCKS * KEYS, DK, 2 * C), BF16),
            pltpu.VMEM((units, C, DV + DK), F32),
            pltpu.VMEM((HEADS, DK, DK), F32),
            pltpu.SemaphoreType.DMA((5,)),
            pltpu.SemaphoreType.DMA((24,)),
        ],
        compiler_params=params(TERMS_MIB),
        cost_estimate=cost(8 * 10**9, 2**25),
        name="terms",
    )(*operands)


def reads_kernel(own, got, halo, taps, *rest):
    sources, (base, reads), kept = rest[: len(KEPT)], rest[len(KEPT) : len(KEPT) + 2], rest[len(KEPT) + 2 : -5]
    bases, readers, raw, staged, sems = rest[-5:]
    core = my_core()
    columns, totals, keys, solved, early_transit, early_add = kept
    copies = []

    def move(source, target, first=None, count=HEADS):
        if first is not None:
            source, target = source.at[first : first + count], target.at[first : first + count]
        copies.append(pltpu.make_async_copy(source, target, sems.at[len(copies)]))
        copies[-1].start()

    move(own.at[:, pl.ds(pl.multiple_of(core * QK, QK), QK)], staged.at[0])
    move(got.at[0:C, 0:QK], staged.at[1])
    for i in (0, 1, 2):
        move(sources[i], kept[i])
    for j in range(BLOCKS):
        move(sources[3], solved, j * HEADS)
        if j == 0:
            move(sources[4], early_transit)
            move(sources[5], early_add)
    inclusive = lax.broadcasted_iota(jnp.int32, (C, C), 0) >= lax.broadcasted_iota(jnp.int32, (C, C), 1)
    for one in copies[:5]:
        one.wait()
    assemble(core, staged, halo, raw, 0, 0, QK)
    for j in range(BLOCKS):
        for one in copies[5:6] if j == 0 else copies[6:9]:
            one.wait()
        for g in range(KEYS):
            queries = convolved(raw, taps, g * DK, core * QK + g * DK, j)
            queries = queries * (over_length(queries) * (1.0 / math.sqrt(DK)))
            qh, ql = split(queries)
            both = keys[j * KEYS + g]
            kh, kl = both[:, :DK], both[:, DK:]
            plain = dot_t(jnp.concatenate([qh, ql], 1), jnp.concatenate([kh, kh], 1)) + dot_t(qh, kl)
            for h in (2 * g, 2 * g + 1):
                u = unit_of(j, h)
                pair = jnp.where(inclusive, jnp.exp(jnp.minimum(column(columns, 0, u) - totals[u : u + 1], 0.0)), 0.0)
                gram = split(pair * plain)
                inner = solved[u]
                out = dot3(gram, (inner[:, :DV], inner[:, DV : 2 * DV]))
                writes = inner[:, 2 * DV : 2 * DV + DK], inner[:, 2 * DV + DK :]
                read = column(columns, 2, u) * queries - dot3(gram, writes)
                if j:
                    high, low = split(read)
                    out = out + dot3((high, low), (early_add[h, :, :DV], early_add[h, :, DV:]))
                    before = unit_of(0, h)
                    read = jnp.exp(totals[before : before + 1, C - 1 : C]) * read - dot(high, early_transit[h])
                bases[u] = out
                high, low = split(read)
                readers[u, :, :DK] = high
                readers[u, :, DK:] = low
        move(bases, base, j * HEADS)
        move(readers, reads, j * HEADS)
    for one in copies[9:]:
        one.wait()


def run_reads(*operands):
    units = BLOCKS * HEADS
    return pl.pallas_call(
        reads_kernel,
        out_shape=[shape((units, C, DV), F32), shape((units, C, 2 * DK), BF16)],
        in_specs=[ANY] * 2 + [VMEM] * 2 + [ANY] * len(KEPT),
        out_specs=[ANY] * 2,
        scratch_shapes=[pltpu.VMEM(*one) for one in KEPT]
        + [
            pltpu.VMEM((units, C, DV), F32),
            pltpu.VMEM((units, C, 2 * DK), BF16),
            pltpu.VMEM((8 + BLOCKS * C, QK), F32),
            pltpu.VMEM((BLOCKS, C, QK), BF16),
            pltpu.SemaphoreType.DMA((15,)),
        ],
        compiler_params=params(TERMS_MIB),
        cost_estimate=cost(4 * 10**9, 2**24),
        name="reads",
    )(*operands)


def enter_kernel(arrived, entering, messages, sems):
    copies = [
        pltpu.make_async_copy(arrived.at[chip], messages.at[chip], sems.at[chip]) for chip in range(CHIPS - 1)
    ]
    for one in copies:
        one.start()
    state = jnp.zeros((DK, DV), F32)
    for chip in range(CHIPS):
        high = state.astype(BF16)
        entering[chip] = high
        if chip < CHIPS - 1:
            copies[chip].wait()
            parts = messages[chip, 2 * DK : WHOLE].astype(F32)
            factor = parts[0:1] + parts[1:2] + parts[2:3]
            state = factor * state - dot(messages[chip, 0:DK], high) + messages[chip, DK : 2 * DK].astype(F32)


def run_enter(messages):
    return pl.pallas_call(
        enter_kernel,
        out_shape=shape((CHIPS, DK, DV), BF16),
        in_specs=[ANY],
        out_specs=VMEM,
        scratch_shapes=[pltpu.VMEM((CHIPS, WHOLE, DV), BF16), pltpu.SemaphoreType.DMA((CHIPS - 1,))],
        compiler_params=params(TERMS_MIB),
        cost_estimate=cost(10**9, 2**20),
        name="enter",
    )(messages)


def finish_kernel(arrived, base, reads, gate, got, gain, mine, theirs, entering, bases, readers, gates, sems):
    core = my_core()
    blocks = 1 - core, core
    loads = [pltpu.make_async_copy(arrived, entering, sems.at[6])]
    loads[0].start()
    for i, block in enumerate(blocks):
        units = pl.ds(pl.multiple_of(block * HEADS, HEADS), HEADS)
        column_of = pl.multiple_of(core * HEADS * DV, HEADS * DV)
        a_gate = gate.at[:, pl.ds(column_of, HEADS * DV)] if i else got.at[0:C, RAW:ROW]
        for source, target in ((a_gate, gates), (reads.at[units], readers), (base.at[units], bases)):
            loads.append(pltpu.make_async_copy(source, target.at[i], sems.at[len(loads) - 1]))
            loads[-1].start()
    for i, out in enumerate((theirs, mine)):
        for one in loads[4:] if i else loads[:4]:
            one.wait()
        for h in range(HEADS):
            state = entering[h]
            rows = bases[i, h] + dot(readers[i, h], jnp.concatenate([state, state], 0))
            square_mean = jnp.mean(rows * rows, -1, keepdims=True)
            opening = silu(gates[i, :, h * DV : (h + 1) * DV].astype(F32))
            out[h] = (rows * lax.rsqrt(square_mean + 1e-06) * gain[...] * opening).astype(BF16)


def run_finish(entering, base, reads, gate, got, gain):
    return pl.pallas_call(
        finish_kernel,
        out_shape=[shape((HEADS, C, DV), BF16)] * 2,
        in_specs=[ANY] * 5 + [VMEM],
        out_specs=[VMEM] * 2,
        scratch_shapes=[
            pltpu.VMEM((HEADS, DK, DV), BF16),
            pltpu.VMEM((BLOCKS, HEADS, C, DV), F32),
            pltpu.VMEM((BLOCKS, HEADS, C, 2 * DK), BF16),
            pltpu.VMEM((BLOCKS, C, HEADS * DV), BF16),
            pltpu.SemaphoreType.DMA((7,)),
        ],
        compiler_params=params(TERMS_MIB),
        cost_estimate=cost(2 * 10**9, 2**22),
        name="finish",
    )(entering, base, reads, gate, got, gain)


def in_order_of(core, heads, ordered):
    row = lax.axis_index("fsdp")
    y, x = row // SIDE, lax.rem(row, SIDE)
    for second in range(SIDE):
        for first in range(SIDE):
            back_x = jnp.where(core == 0, first, second)
            back_y = jnp.where(core == 0, second, first)
            head = lax.rem(y - back_y + SIDE, SIDE) * SIDE + lax.rem(x - back_x + SIDE, SIDE)
            at = (second * SIDE + first) * DV
            ordered[:, at : at + DV] = heads[head]


def product_of(ordered, weights):
    width = SIDE * DV
    total = dot(ordered[:, :width], weights[0][...].reshape(width, HALF))
    for second in range(1, SIDE):
        at = second * width
        total = total + dot(ordered[:, at : at + width], weights[second][...].reshape(width, HALF))
    return total.astype(BF16)


def project_kernel(mine, theirs, *rest):
    own, others, (out, normed, ordered) = rest[:SIDE], rest[SIDE : 2 * SIDE], rest[2 * SIDE :]
    core = my_core()
    for source, its_core in ((mine, core), (theirs, 1 - core)):
        normed[pl.ds(its_core * HEADS, HEADS)] = source[...]
    for its_core, weights in ((core, own), (1 - core, others)):
        in_order_of(its_core, normed, ordered)
        out[:, pl.ds(pl.multiple_of(its_core * HALF, HALF), HALF)] = product_of(ordered, weights)


def project(mine, theirs, weights, other_weights):
    return pl.pallas_call(
        project_kernel,
        out_shape=shape((C, WIDTH), BF16),
        in_specs=[VMEM] * (2 + 2 * SIDE),
        out_specs=VMEM,
        compiler_params=params(40),
        cost_estimate=cost(2 * C * WIDTH * WIDTH, 2**23),
        scratch_shapes=[
            pltpu.VMEM((VH, C, DV), BF16),
            pltpu.VMEM((C, WIDTH), BF16),
        ],
        name="project",
    )(mine, theirs, *weights, *other_weights)


def along(block, distance, second):
    route = []
    for i in range(SEGMENTS):
        by_x = (i % 2 == 0) != second
        for y in range(SIDE):
            for x in range(SIDE):
                to_y, to_x = (y, (x + distance) % SIDE) if by_x else ((y + distance) % SIDE, x)
                route.append(((i * SIDE + y) * SIDE + x, (i * SIDE + to_y) * SIDE + to_x))
    return lax.ppermute(block, ("seq", "fsdp"), route)


def local(
    qkv_raw,
    output_gate,
    decay_codes,
    beta_codes,
    conv_weight,
    decay_scale_log,
    decay_bias,
    norm_gain,
    out_weight,
):
    barrier = lax.optimization_barrier
    raw, decay, beta = qkv_raw[0], decay_codes[0], beta_codes[0]
    give, tail, half = cut_rows(raw, output_gate[0], decay, beta, out_weight)
    got = other_core(give)
    tail = jnp.where(lax.axis_index("seq") % 2 == 0, got[C - 16 : C, :RAW], tail)
    halo = lax.ppermute(tail, "seq", [(i, i + 2) for i in range(SEGMENTS - 2)])
    parts = [along(half, distance, False) for distance in (1, 2, 3)]
    message, *kept = run_terms(
        decay_scale_log, decay_bias, decay, beta, raw, got, halo, conv_weight
    )
    message, half, *parts = barrier((message, half, *parts))
    messages = between_chips(message)
    line = jnp.stack([half, *parts])
    later = [along(line, distance, True) for distance in (1, 2, 3)]
    other_line = other_core(line)
    base, reads = run_reads(raw, got, halo, conv_weight, *kept)
    messages, base, reads = barrier((messages, base, reads))
    entering = between_chips(run_enter(messages))
    entering, *later = barrier((entering, *later))
    other_weights = [other_line] + [other_core(weight) for weight in later]
    mine, theirs = run_finish(entering, base, reads, output_gate[0], got, norm_gain[None])
    return project(mine, other_core(theirs), [line, *later], other_weights)[None]


def solution(mesh):
    return jax.shard_map(
        local,
        mesh=mesh,
        in_specs=(
            P("fsdp", "seq", None),
            P("fsdp", "seq", None),
            P("fsdp", None, "seq"),
            P("fsdp", None, "seq"),
            P(),
            P(),
            P(),
            P(),
            P("fsdp", None),
        ),
        out_specs=P("fsdp", "seq", None),
        check_vma=False,
    )
```

```python
import math

import jax
import jax.numpy as jnp
from jax import lax
from jax.experimental import pallas as pl
from jax.experimental.pallas import tpu as pltpu
from jax.sharding import PartitionSpec as P


CHIPS = 8
SEGMENTS = 16
C = 128
DK = 128
DV = 128
VH = 16
HEADS = 8
KEYS = 4
BLOCKS = 2
WIDTH = 2048
HALF = 1024
QK = KEYS * DK
RAW = 2 * QK + HEADS * DV
ROW = RAW + HEADS * DV
TALL = C + 16
TERMS_MIB = 60
WHOLE = 2 * DK + 16
SIDE = 4
F32 = jnp.float32
BF16 = jnp.bfloat16
VMEM = pl.BlockSpec(memory_space=pltpu.VMEM)
SMEM = pl.BlockSpec(memory_space=pltpu.SMEM)


def to_chip(block, distance):
    return lax.ppermute(
        block, "seq", [(i, (i + 2 * distance) % SEGMENTS) for i in range(SEGMENTS)]
    )


def other_core(block):
    return lax.ppermute(block, "seq", [(i, i ^ 1) for i in range(SEGMENTS)])


def between_chips(blocks):
    groups = [[2 * z + c for z in range(CHIPS)] for c in range(2)]
    return lax.all_to_all(blocks, "seq", 0, 0, axis_index_groups=groups)


def dot(left, right):
    return jnp.dot(left, right, preferred_element_type=F32)


def dot_t(left, right):
    return lax.dot_general(
        left, right, (((1,), (1,)), ((), ())), preferred_element_type=F32
    )


def split(value):
    high = value.astype(BF16)
    return high, (value - high.astype(F32)).astype(BF16)


def dot3(left, right):
    lh, ll = left
    rh, rl = right
    return dot(jnp.concatenate([lh, ll], 1), jnp.concatenate([rh, rh], 0)) + dot(lh, rl)


def silu(value):
    return value / (1.0 + jnp.exp(-value))


ANY = pl.BlockSpec(memory_space=pl.ANY)
KEPT = (
    ((C, C), F32),
    ((BLOCKS * HEADS, C), F32),
    ((BLOCKS * KEYS, C, 2 * DK), BF16),
    ((BLOCKS * HEADS, C, 2 * DV + 2 * DK), BF16),
    ((HEADS, DK, DK), BF16),
    ((HEADS, DK, 2 * DV), BF16),
)


def shape(dims, kind):
    return jax.ShapeDtypeStruct(dims, kind)


def my_core():
    return lax.rem(lax.axis_index("seq"), 2)


def params(mib):
    return pltpu.CompilerParams(vmem_limit_bytes=mib * 2**20)


def cost(flops, moved):
    return pl.CostEstimate(flops=flops, bytes_accessed=moved, transcendentals=0)


def cut_kernel(raw, gate, decay, beta, weight, give, tail, half, rows, decays, betas, sems):
    core = my_core()
    copies = []

    def copy(source, target):
        copies.append(pltpu.make_async_copy(source, target, sems.at[len(copies)]))
        copies[-1].start()

    def cut(ref, first, width, part, at=0, count=C):
        column = pl.multiple_of(first + part * width, width)
        return ref.at[at : at + count, pl.ds(column, width)]

    copy(decay, decays)
    copy(beta, betas)
    parts = ((0, QK, 0), (2 * QK, QK, QK), (4 * QK, HEADS * DV, 2 * QK))
    for first, width, to in parts:
        copy(cut(raw, first, width, 1 - core), give.at[0:C, to : to + width])
    copy(cut(gate, 0, HEADS * DV, 1 - core), give.at[0:C, RAW:ROW])
    for first, width, to in parts:
        copy(cut(raw, first, width, core, C - 16, 16), tail.at[:, to : to + width])
    copy(cut(weight, 0, HALF, core), half)
    give[C:TALL, 2 * C :] = jnp.zeros((16, ROW - 2 * C), BF16)
    copies[0].wait()
    copies[1].wait()
    for at, codes in ((0, decays), (C, betas)):
        code = codes[pl.ds(pl.multiple_of((1 - core) * HEADS, HEADS), HEADS), :]
        rows[0:HEADS, at : at + C] = (code >> 4).astype(F32)
        rows[HEADS:16, at : at + C] = (code & 15).astype(F32)
    give[C:TALL, 0 : 2 * C] = rows[...].astype(BF16)
    for one in copies[2:]:
        one.wait()


def cut_rows(raw, gate, decay, beta, weight):
    return pl.pallas_call(
        cut_kernel,
        out_shape=[
            shape((TALL, ROW), BF16),
            shape((16, RAW), BF16),
            shape((weight.shape[0], HALF), BF16),
        ],
        in_specs=[ANY] * 5,
        out_specs=[VMEM] * 3,
        scratch_shapes=[
            pltpu.VMEM((16, 2 * C), F32),
            pltpu.VMEM((VH, C), jnp.int32),
            pltpu.VMEM((VH, C), jnp.int32),
            pltpu.SemaphoreType.DMA((10,)),
        ],
        compiler_params=params(60),
        name="cut",
    )(raw, gate, decay, beta, weight)


def assemble(core, staged, halo, raw, first, at, width):
    to = slice(at, at + width)
    raw[0:8, to] = halo[:, first + at : first + at + width].astype(F32)[8:16]
    for i, block in enumerate((core, 1 - core)):
        raw[pl.ds(pl.multiple_of(8 + block * C, 8), C), to] = staged[i, :, to].astype(F32)


def convolved(raw, taps, at, channel, j):
    weights = taps[:, pl.ds(pl.multiple_of(channel, DK), DK)]
    base = 8 + j * C - 3
    total = weights[0:1] * raw[base : base + C, at : at + DK]
    for t in range(1, 4):
        total = total + weights[t : t + 1] * raw[base + t : base + t + C, at : at + DK]
    return silu(total)


def over_length(value):
    return lax.rsqrt(jnp.sum(value * value, -1, keepdims=True) + 1e-06)


def unit_of(j, h):
    return j * HEADS + h


def column(columns, kind, unit):
    at = kind * BLOCKS * HEADS + unit
    return columns[:, at : at + 1]


def terms_kernel(
    scale_log, bias, decay_codes, beta_codes, own, got, halo, taps,
    message, *rest,
):
    outs, kept, rest = rest[: len(KEPT)], rest[len(KEPT) : 2 * len(KEPT)], rest[2 * len(KEPT) :]
    raw, staged, their_codes, decay, beta, joins, keys_t, rights, transit, arrive, sems = rest
    columns, totals, keys_out, solved_out, early_transit, early_add = kept
    core = my_core()
    copies = []
    column_of = pl.multiple_of(2 * QK + core * QK, QK), pl.multiple_of(4 * QK + core * HEADS * DV, HEADS * DV)
    loads = [
        pltpu.make_async_copy(*one, arrive.at[i])
        for i, one in enumerate((
            (got.at[C:TALL, 0 : 2 * C], their_codes),
            (own.at[:, pl.ds(column_of[0], QK)], staged.at[0, :, 0:QK]),
            (got.at[0:C, QK : 2 * QK], staged.at[1, :, 0:QK]),
            (own.at[:, pl.ds(column_of[1], HEADS * DV)], staged.at[0, :, QK:]),
            (got.at[0:C, 2 * QK : RAW], staged.at[1, :, QK:]),
        ))
    ]
    for one in loads:
        one.start()

    def leave(which, first=0, count=None):
        source, target = kept[which], outs[which]
        if count:
            source, target = source.at[first : first + count], target.at[first : first + count]
        copies.append(pltpu.make_async_copy(source, target, sems.at[len(copies)]))
        copies[-1].start()

    loads[0].wait()
    codes = their_codes[...].astype(F32)
    ours = pl.ds(pl.multiple_of(core * HEADS, HEADS), HEADS)
    theirs = pl.ds(pl.multiple_of((1 - core) * HEADS, HEADS), HEADS)
    decay[ours, :] = decay_codes[ours, :].astype(F32)
    beta[ours, :] = beta_codes[ours, :].astype(F32)
    decay[theirs, :] = 16.0 * codes[0:HEADS, 0:C] + codes[HEADS:16, 0:C]
    beta[theirs, :] = 16.0 * codes[0:HEADS, C:] + codes[HEADS:16, C:]

    def by_head(ref):
        rows = [jnp.full((1, C), ref[core * HEADS + h], F32) for h in range(HEADS)]
        return jnp.concatenate(rows * BLOCKS, 0)

    level = decay[...] / 32.0 - 16.0 + by_head(bias)
    small = jnp.exp(-jnp.abs(level))
    one_more = 1.0 + small
    gap = one_more - 1.0
    log1p = jnp.where(gap == 0.0, small, jnp.log(one_more) * (small / jnp.where(gap == 0.0, 1.0, gap)))
    log_decay = -jnp.exp(by_head(scale_log)) * (jnp.maximum(level, 0.0) + log1p)
    row_ids = lax.broadcasted_iota(jnp.int32, (C, C), 0)
    col_ids = lax.broadcasted_iota(jnp.int32, (C, C), 1)
    sums = jnp.dot(
        log_decay,
        (row_ids <= col_ids).astype(F32),
        precision=lax.Precision.HIGHEST,
        preferred_element_type=F32,
    )
    strength = 1.0 / (1.0 + jnp.exp(8.0 - beta[...] / 32.0))
    start = jnp.exp(sums)
    totals[...] = sums
    end = jnp.exp(sums[:, C - 1 : C] - sums)
    columns[...] = jnp.concatenate(
        [sums, strength, start, end, strength * start, jnp.zeros((C - 5 * BLOCKS * HEADS, C), F32)], 0
    ).T

    leave(0)
    leave(1)
    inclusive = row_ids >= col_ids
    strict = row_ids > col_ids
    eye = (row_ids == col_ids).astype(BF16)
    for k in range(1, 7):
        joins[k - 1] = (
            ((row_ids >> (k + 1)) == (col_ids >> (k + 1))) & ((row_ids >> k) != (col_ids >> k))
        ).astype(F32).astype(BF16)
    near = (row_ids >> 1) == (col_ids >> 1)

    for one in loads[1:3]:
        one.wait()
    assemble(core, staged, halo, raw, QK, 0, QK)
    units = range(BLOCKS * HEADS)
    lowers, inverses = [], []
    for j in range(BLOCKS):
        for g in range(KEYS):
            keys = convolved(raw, taps, g * DK, 2 * QK + core * QK + g * DK, j)
            keys = keys * over_length(keys)
            kh, kl = split(keys)
            keys_out[j * KEYS + g, :, :DK] = kh
            keys_out[j * KEYS + g, :, DK:] = kl
            kh_t, kl_t = split(keys.T)
            keys_t[j * KEYS + g, :, :C] = kh_t
            keys_t[j * KEYS + g, :, C:] = kl_t
            gram = dot_t(kh, kh)
            for h in (2 * g, 2 * g + 1):
                u = unit_of(j, h)
                pair = jnp.where(inclusive, jnp.exp(jnp.minimum(column(columns, 0, u) - sums[u : u + 1], 0.0)), 0.0)
                lower = jnp.where(strict, column(columns, 1, u) * pair * gram, 0.0)
                lowers.append(lower.astype(BF16))
                inverses.append(eye - jnp.where(near, lower, 0.0).astype(BF16))
                rights[u, :, DV:] = column(columns, 4, u) * keys
        leave(2, j * KEYS, KEYS)
    for one in loads[3:]:
        one.wait()
    assemble(core, staged, halo, raw, QK, QK, HEADS * DV)
    for k in range(6):
        for u in units[3 * k : 3 * k + 3]:
            j, h = u // HEADS, u % HEADS
            values = convolved(raw, taps, QK + h * DV, 4 * QK + core * HEADS * DV + h * DV, j)
            rights[u, :, :DV] = column(columns, 1, u) * values
        halves = [dot(lowers[u] * joins[k], inverses[u]).astype(BF16) for u in units]
        inverses = [inverses[u] - dot(inverses[u], halves[u]).astype(BF16) for u in units]
    for u in units:
        j, h = u // HEADS, u % HEADS
        solved = rights[u] + dot(inverses[u] - eye, rights[u].astype(BF16))
        values, writes = solved[:, :DV], solved[:, DV:]
        high, low = split(values)
        solved_out[u, :, :DV] = high
        solved_out[u, :, DV : 2 * DV] = low
        high, low = split(writes)
        solved_out[u, :, 2 * DV : 2 * DV + DK] = high
        solved_out[u, :, 2 * DV + DK :] = low
        leave(3, u, 1)
        g = j * KEYS + h // 2
        kt = keys_t[g, :, :C], keys_t[g, :, C:]
        moved = dot3(kt, split(column(columns, 3, u) * writes))
        add = dot3(kt, split(column(columns, 3, u) * values))
        last = start[u : u + 1, C - 1 : C]
        if j == 0:
            transit[h] = moved
            early_transit[h] = moved.astype(BF16)
            add_high, add_low = split(add)
            early_add[h, :, :DV] = add_high
            early_add[h, :, DV:] = add_low
        else:
            first = start[unit_of(0, h) : unit_of(0, h) + 1, C - 1 : C]
            second = moved.astype(BF16)
            crossed = dot(second, jnp.concatenate([early_transit[h], early_add[h, :, :DV]], 1))
            earlier = early_add[h, :, :DV].astype(F32) + early_add[h, :, DV:].astype(F32)
            message[h, 0:DK] = (last * transit[h] + first * moved - crossed[:, :DK]).astype(BF16)
            message[h, DK : 2 * DK] = (last * earlier - crossed[:, DK:] + add).astype(BF16)
            both = jnp.broadcast_to(first * last, (1, DK))
            top = both.astype(BF16).astype(F32)
            middle = (both - top).astype(BF16).astype(F32)
            parts = jnp.concatenate([top, middle, both - top - middle, jnp.zeros((13, DK), F32)], 0)
            message[h, 2 * DK : WHOLE] = parts.astype(BF16)
        if u == HEADS - 1:
            leave(4)
            leave(5)
    for one in copies:
        one.wait()


def run_terms(*operands):
    units = BLOCKS * HEADS
    return pl.pallas_call(
        terms_kernel,
        out_shape=[shape((HEADS, WHOLE, DV), BF16)] + [shape(*one) for one in KEPT],
        in_specs=[SMEM] * 2 + [VMEM] * 2 + [ANY] * 2 + [VMEM] * 2,
        out_specs=[VMEM] + [ANY] * len(KEPT),
        scratch_shapes=[pltpu.VMEM(*one) for one in KEPT]
        + [
            pltpu.VMEM((8 + BLOCKS * C, RAW - QK), F32),
            pltpu.VMEM((BLOCKS, C, RAW - QK), BF16),
            pltpu.VMEM((16, 2 * C), BF16),
            pltpu.VMEM((units, C), F32),
            pltpu.VMEM((units, C), F32),
            pltpu.VMEM((6, C, C), BF16),
            pltpu.VMEM((BLOCKS * KEYS, DK, 2 * C), BF16),
            pltpu.VMEM((units, C, DV + DK), F32),
            pltpu.VMEM((HEADS, DK, DK), F32),
            pltpu.SemaphoreType.DMA((5,)),
            pltpu.SemaphoreType.DMA((24,)),
        ],
        compiler_params=params(TERMS_MIB),
        cost_estimate=cost(8 * 10**9, 2**25),
        name="terms",
    )(*operands)


def reads_kernel(own, got, halo, taps, *rest):
    sources, (base, reads), kept = rest[: len(KEPT)], rest[len(KEPT) : len(KEPT) + 2], rest[len(KEPT) + 2 : -5]
    bases, readers, raw, staged, sems = rest[-5:]
    core = my_core()
    columns, totals, keys, solved, early_transit, early_add = kept
    copies = []

    def move(source, target, first=None, count=HEADS):
        if first is not None:
            source, target = source.at[first : first + count], target.at[first : first + count]
        copies.append(pltpu.make_async_copy(source, target, sems.at[len(copies)]))
        copies[-1].start()

    move(own.at[:, pl.ds(pl.multiple_of(core * QK, QK), QK)], staged.at[0])
    move(got.at[0:C, 0:QK], staged.at[1])
    for i in (0, 1, 2):
        move(sources[i], kept[i])
    for j in range(BLOCKS):
        move(sources[3], solved, j * HEADS)
        if j == 0:
            move(sources[4], early_transit)
            move(sources[5], early_add)
    inclusive = lax.broadcasted_iota(jnp.int32, (C, C), 0) >= lax.broadcasted_iota(jnp.int32, (C, C), 1)
    for one in copies[:5]:
        one.wait()
    assemble(core, staged, halo, raw, 0, 0, QK)
    for j in range(BLOCKS):
        for one in copies[5:6] if j == 0 else copies[6:9]:
            one.wait()
        for g in range(KEYS):
            queries = convolved(raw, taps, g * DK, core * QK + g * DK, j)
            queries = queries * (over_length(queries) * (1.0 / math.sqrt(DK)))
            qh, ql = split(queries)
            both = keys[j * KEYS + g]
            kh, kl = both[:, :DK], both[:, DK:]
            plain = dot_t(jnp.concatenate([qh, ql], 1), jnp.concatenate([kh, kh], 1)) + dot_t(qh, kl)
            for h in (2 * g, 2 * g + 1):
                u = unit_of(j, h)
                pair = jnp.where(inclusive, jnp.exp(jnp.minimum(column(columns, 0, u) - totals[u : u + 1], 0.0)), 0.0)
                gram = split(pair * plain)
                inner = solved[u]
                out = dot3(gram, (inner[:, :DV], inner[:, DV : 2 * DV]))
                writes = inner[:, 2 * DV : 2 * DV + DK], inner[:, 2 * DV + DK :]
                read = column(columns, 2, u) * queries - dot3(gram, writes)
                if j:
                    high, low = split(read)
                    out = out + dot3((high, low), (early_add[h, :, :DV], early_add[h, :, DV:]))
                    before = unit_of(0, h)
                    read = jnp.exp(totals[before : before + 1, C - 1 : C]) * read - dot(high, early_transit[h])
                bases[u] = out
                high, low = split(read)
                readers[u, :, :DK] = high
                readers[u, :, DK:] = low
        move(bases, base, j * HEADS)
        move(readers, reads, j * HEADS)
    for one in copies[9:]:
        one.wait()


def run_reads(*operands):
    units = BLOCKS * HEADS
    return pl.pallas_call(
        reads_kernel,
        out_shape=[shape((units, C, DV), F32), shape((units, C, 2 * DK), BF16)],
        in_specs=[ANY] * 2 + [VMEM] * 2 + [ANY] * len(KEPT),
        out_specs=[ANY] * 2,
        scratch_shapes=[pltpu.VMEM(*one) for one in KEPT]
        + [
            pltpu.VMEM((units, C, DV), F32),
            pltpu.VMEM((units, C, 2 * DK), BF16),
            pltpu.VMEM((8 + BLOCKS * C, QK), F32),
            pltpu.VMEM((BLOCKS, C, QK), BF16),
            pltpu.SemaphoreType.DMA((15,)),
        ],
        compiler_params=params(TERMS_MIB),
        cost_estimate=cost(4 * 10**9, 2**24),
        name="reads",
    )(*operands)


def enter_kernel(arrived, entering, messages, sems):
    copies = [
        pltpu.make_async_copy(arrived.at[chip], messages.at[chip], sems.at[chip]) for chip in range(CHIPS - 1)
    ]
    for one in copies:
        one.start()
    state = jnp.zeros((DK, DV), F32)
    for chip in range(CHIPS):
        high = state.astype(BF16)
        entering[chip] = high
        if chip < CHIPS - 1:
            copies[chip].wait()
            parts = messages[chip, 2 * DK : WHOLE].astype(F32)
            factor = parts[0:1] + parts[1:2] + parts[2:3]
            state = factor * state - dot(messages[chip, 0:DK], high) + messages[chip, DK : 2 * DK].astype(F32)


def run_enter(messages):
    return pl.pallas_call(
        enter_kernel,
        out_shape=shape((CHIPS, DK, DV), BF16),
        in_specs=[ANY],
        out_specs=VMEM,
        scratch_shapes=[pltpu.VMEM((CHIPS, WHOLE, DV), BF16), pltpu.SemaphoreType.DMA((CHIPS - 1,))],
        compiler_params=params(TERMS_MIB),
        cost_estimate=cost(10**9, 2**20),
        name="enter",
    )(messages)


def finish_kernel(arrived, base, reads, gate, got, gain, mine, theirs, entering, bases, readers, gates, sems):
    core = my_core()
    blocks = 1 - core, core
    loads = [pltpu.make_async_copy(arrived, entering, sems.at[6])]
    loads[0].start()
    for i, block in enumerate(blocks):
        units = pl.ds(pl.multiple_of(block * HEADS, HEADS), HEADS)
        column_of = pl.multiple_of(core * HEADS * DV, HEADS * DV)
        a_gate = gate.at[:, pl.ds(column_of, HEADS * DV)] if i else got.at[0:C, RAW:ROW]
        for source, target in ((a_gate, gates), (reads.at[units], readers), (base.at[units], bases)):
            loads.append(pltpu.make_async_copy(source, target.at[i], sems.at[len(loads) - 1]))
            loads[-1].start()
    for i, out in enumerate((theirs, mine)):
        for one in loads[4:] if i else loads[:4]:
            one.wait()
        for h in range(HEADS):
            state = entering[h]
            rows = bases[i, h] + dot(readers[i, h], jnp.concatenate([state, state], 0))
            square_mean = jnp.mean(rows * rows, -1, keepdims=True)
            opening = silu(gates[i, :, h * DV : (h + 1) * DV].astype(F32))
            out[h] = (rows * lax.rsqrt(square_mean + 1e-06) * gain[...] * opening).astype(BF16)


def run_finish(entering, base, reads, gate, got, gain):
    return pl.pallas_call(
        finish_kernel,
        out_shape=[shape((HEADS, C, DV), BF16)] * 2,
        in_specs=[ANY] * 5 + [VMEM],
        out_specs=[VMEM] * 2,
        scratch_shapes=[
            pltpu.VMEM((HEADS, DK, DV), BF16),
            pltpu.VMEM((BLOCKS, HEADS, C, DV), F32),
            pltpu.VMEM((BLOCKS, HEADS, C, 2 * DK), BF16),
            pltpu.VMEM((BLOCKS, C, HEADS * DV), BF16),
            pltpu.SemaphoreType.DMA((7,)),
        ],
        compiler_params=params(55),
        cost_estimate=cost(2 * 10**9, 2**22),
        name="finish",
    )(entering, base, reads, gate, got, gain)


def in_order_of(core, heads, ordered):
    row = lax.axis_index("fsdp")
    y, x = row // SIDE, lax.rem(row, SIDE)
    for second in range(SIDE):
        for first in range(SIDE):
            back_x = jnp.where(core == 0, first, second)
            back_y = jnp.where(core == 0, second, first)
            head = lax.rem(y - back_y + SIDE, SIDE) * SIDE + lax.rem(x - back_x + SIDE, SIDE)
            at = (second * SIDE + first) * DV
            ordered[:, at : at + DV] = heads[head]


def product_of(ordered, weights):
    width = SIDE * DV
    total = dot(ordered[:, :width], weights[0][...].reshape(width, HALF))
    for second in range(1, SIDE):
        at = second * width
        total = total + dot(ordered[:, at : at + width], weights[second][...].reshape(width, HALF))
    return total.astype(BF16)


def project_kernel(mine, theirs, *rest):
    own, others, (out, normed, ordered) = rest[:SIDE], rest[SIDE : 2 * SIDE], rest[2 * SIDE :]
    core = my_core()
    for source, its_core in ((mine, core), (theirs, 1 - core)):
        normed[pl.ds(its_core * HEADS, HEADS)] = source[...]
    for its_core, weights in ((core, own), (1 - core, others)):
        in_order_of(its_core, normed, ordered)
        out[:, pl.ds(pl.multiple_of(its_core * HALF, HALF), HALF)] = product_of(ordered, weights)


def project(mine, theirs, weights, other_weights):
    return pl.pallas_call(
        project_kernel,
        out_shape=shape((C, WIDTH), BF16),
        in_specs=[VMEM] * (2 + 2 * SIDE),
        out_specs=VMEM,
        compiler_params=params(24),
        cost_estimate=cost(2 * C * WIDTH * WIDTH, 2**23),
        scratch_shapes=[
            pltpu.VMEM((VH, C, DV), BF16),
            pltpu.VMEM((C, WIDTH), BF16),
        ],
        name="project",
    )(mine, theirs, *weights, *other_weights)


def along(block, distance, second):
    route = []
    for i in range(SEGMENTS):
        by_x = (i % 2 == 0) != second
        for y in range(SIDE):
            for x in range(SIDE):
                to_y, to_x = (y, (x + distance) % SIDE) if by_x else ((y + distance) % SIDE, x)
                route.append(((i * SIDE + y) * SIDE + x, (i * SIDE + to_y) * SIDE + to_x))
    return lax.ppermute(block, ("seq", "fsdp"), route)


def local(
    qkv_raw,
    output_gate,
    decay_codes,
    beta_codes,
    conv_weight,
    decay_scale_log,
    decay_bias,
    norm_gain,
    out_weight,
):
    barrier = lax.optimization_barrier
    raw, decay, beta = qkv_raw[0], decay_codes[0], beta_codes[0]
    give, tail, half = cut_rows(raw, output_gate[0], decay, beta, out_weight)
    got = other_core(give)
    tail = jnp.where(lax.axis_index("seq") % 2 == 0, got[C - 16 : C, :RAW], tail)
    halo = lax.ppermute(tail, "seq", [(i, i + 2) for i in range(SEGMENTS - 2)])
    parts = [along(half, distance, False) for distance in (1, 2, 3)]
    message, *kept = run_terms(
        decay_scale_log, decay_bias, decay, beta, raw, got, halo, conv_weight
    )
    message, half, *parts = barrier((message, half, *parts))
    messages = between_chips(message)
    line = jnp.stack([half, *parts])
    later = [along(line, distance, True) for distance in (1, 2, 3)]
    other_line = other_core(line)
    base, reads = run_reads(raw, got, halo, conv_weight, *kept)
    messages, base, reads = barrier((messages, base, reads))
    entering = between_chips(run_enter(messages))
    entering, *later = barrier((entering, *later))
    other_weights = [other_line] + [other_core(weight) for weight in later]
    mine, theirs = run_finish(entering, base, reads, output_gate[0], got, norm_gain[None])
    return project(mine, other_core(theirs), [line, *later], other_weights)[None]


def solution(mesh):
    return jax.shard_map(
        local,
        mesh=mesh,
        in_specs=(
            P("fsdp", "seq", None),
            P("fsdp", "seq", None),
            P("fsdp", None, "seq"),
            P("fsdp", None, "seq"),
            P(),
            P(),
            P(),
            P(),
            P("fsdp", None),
        ),
        out_specs=P("fsdp", "seq", None),
        check_vma=False,
    )
```
